32 devices in a mesh: dp: 8 (over y, x, core), tensor: 4 (over z).
Axes of the slice: x: 2, y: 2, z: 4, core: 2. Of those that a mesh axis runs over, the one named last changes fastest.
Arguments:
- tokens: bfloat16 [16384, 768], P('dp'), may hold values from -6 to 6
- projections: bfloat16 [3, 768, 768], P(None, None, 'tensor'), may hold values from -0.21875 to 0.21875
- query_bias: float32 [768], P('tensor'), may hold values from -3 to 3
- value_bias: float32 [768], P('tensor'), may hold values from -0.3 to 0.3
- mixer: bfloat16 [768, 768], P('tensor'), may hold values from -1.75 to 1.75
- mixer_bias: float32 [768], replicated, may hold values from -3 to 3
- first_gain: float32 [768], replicated, may hold values from 0.1 to 1.9
- first_shift: float32 [768], replicated, may hold values from -3 to 3
- up_weight: bfloat16 [768, 3072], P(None, 'tensor'), may hold values from -0.21875 to 0.21875
- up_bias: float32 [3072], P('tensor'), may hold values from -3 to 3
- down_weight: bfloat16 [3072, 768], P('tensor'), may hold values from -0.109375 to 0.109375
- down_bias: float32 [768], replicated, may hold values from -2 to 2
- second_gain: float32 [768], replicated, may hold values from 0.1 to 1.9
- second_shift: float32 [768], replicated, may hold values from -3 to 3
- lengths: int32 [32], P('dp'), may hold values from 0 to 2048, as said below
- cotangent: bfloat16 [16384, 768], P('dp'), may hold values from -6 to 6
Outputs:
- layer_output: bfloat16 [16384, 768], P(('dp', 'tensor'))
- tokens_gradient: float32 [16384, 768], P(('dp', 'tensor'))
- projections_gradient: float32 [3, 768, 768], P(None, 'dp', 'tensor')
- query_bias_gradient: float32 [768], P('tensor')
- value_bias_gradient: float32 [768], P('tensor')
- mixer_gradient: float32 [768, 768], P('tensor', 'dp')
- mixer_bias_gradient: float32 [768], replicated
- first_gain_gradient: float32 [768], replicated
- first_shift_gradient: float32 [768], replicated
- up_weight_gradient: float32 [768, 3072], P('dp', 'tensor')
- up_bias_gradient: float32 [3072], P('tensor')
- down_weight_gradient: float32 [3072, 768], P('tensor', 'dp')
- down_bias_gradient: float32 [768], replicated
- second_gain_gradient: float32 [768], replicated
- second_shift_gradient: float32 [768], replicated
The draws below stay inside these ranges and needn't reach their ends.
Inputs may be any that keep to these rules, and one draw needn't show every extreme that they name: In each block of 4 lengths the lengths sum to at most 2048 and the first is 512 or more; in some block the first length is exactly 2048.
All inputs are finite; a program needn't handle non-finite values.
Results may differ from the reference program's by a relative error of at most 0.019.
Values may be sent and summed in bfloat16 or wider, within the bound.
No kernel may reach another device: no remote copies, remote signals or barrier semaphores. Data moves between devices by JAX's collectives and lax.ppermute only.
A program may use at most 192 MiB of HBM per device.

```python
import jax
import jax.numpy as jnp
from jax import lax

HEADS = 12
HEAD_DIM = 64
D = 768
FF = 3072
TOK_DEV = 2048
LMAX = 2048
SLOTS = 4
TOKENS = 16384
N_DP = 8
N_TENSOR = 4


def draw_lengths(key, part):
    key = jax.random.fold_in(key, 11)
    first_key, rest_key, full_key = jax.random.split(key, 3)
    first = jax.random.randint(first_key, (N_DP, 1), LMAX // 4, 3 * LMAX // 4 + 1)
    chosen = jax.random.randint(full_key, (), 0, N_DP)
    first = jnp.where(jnp.arange(N_DP)[:, None] == chosen, LMAX, first).astype(jnp.int32)
    room = TOK_DEV - first
    rest_top = jnp.minimum(room // (SLOTS - 1), LMAX).astype(jnp.int32)
    units = jax.random.randint(rest_key, (N_DP, SLOTS - 1), 0, 65536)
    rest = (units * (rest_top + 1) // 65536).astype(jnp.int32)
    return jnp.concatenate([first, rest], axis=1).reshape(N_DP * SLOTS).astype(jnp.int32)


def raised(values, rng, source, target, shards_of, factor):
    def block_of(position):
        return (jnp.arange(values.shape[position]) // (values.shape[position] // shards_of)).reshape((-1,) + (1,) * (values.ndim - 1 - position))

    one_side = jax.random.permutation(rng, shards_of)[block_of(target)]
    far = (block_of(target) + shards_of // 2) % shards_of
    return jnp.where((block_of(source) == one_side) | (block_of(source) == far), factor * values, values)


def shard_levels(own_key, dims, pieces, least, top_value):
    def one(axis_at, parts):
        draws = jax.random.uniform(jax.random.fold_in(jax.random.fold_in(own_key, 6), axis_at), (parts,), jnp.float32, least / len(pieces), top_value / len(pieces))
        return jnp.repeat(jnp.exp(draws), dims[axis_at] // parts).reshape((-1,) + (1,) * (len(dims) - axis_at - 1))

    factor_of = one(*pieces[0])
    for cut in pieces[1:]:
        factor_of = factor_of * one(*cut)
    return factor_of


def scatter_about(key, extent, width, most, shards=(), kind=jnp.bfloat16):
    values = width * jax.random.normal(key, extent, jnp.float32)
    if shards:
        values = values * shard_levels(key, extent, shards, -0.22, 0.18)
    return jnp.clip(values, -most, most).astype(kind)


def noise_with(key, extent, deviation, most, cuts, heavy, held_as=jnp.bfloat16):
    values = deviation * jax.random.normal(key, extent, jnp.float32)
    if cuts:
        values = values * shard_levels(key, extent, cuts, -0.22, 0.18)
    return jnp.clip(raised(values, jax.random.fold_in(key, 3), *heavy), -most, most).astype(held_as)


def setup_inputs(seed: int = 0) -> dict:
    key_list = jax.random.split(jax.random.key(seed), 17)
    return {
        "tokens": scatter_about(key_list[0], (TOKENS, D), 1.0, 6.0, ((0, 8),)),
        "projections": scatter_about(key_list[1], (3, D, D), D ** -0.5, 0.21875, ((2, 4),)),
        "query_bias": scatter_about(key_list[2], (D,), 0.5, 3.0, ((0, 4),), jnp.float32),
        "value_bias": scatter_about(key_list[3], (D,), 0.05, 0.3, ((0, 4),), jnp.float32),
        "mixer": scatter_about(key_list[4], (D, D), (max(D // 64, 1)) ** -0.5, 1.75, ((0, 4),)),
        "mixer_bias": scatter_about(key_list[5], (D,), 0.5, 3.0, (), jnp.float32),
        "first_gain": jnp.clip(1.0 + 0.18 * jax.random.normal(key_list[6], (D,), jnp.float32), 0.1, 1.9),
        "first_shift": scatter_about(key_list[7], (D,), 0.5, 3.0, (), jnp.float32),
        "up_weight": scatter_about(key_list[8], (D, FF), D ** -0.5, 0.21875, ((1, 4),)),
        "up_bias": scatter_about(key_list[9], (FF,), 0.5, 3.0, ((0, 4),), jnp.float32),
        "down_weight": scatter_about(key_list[10], (FF, D), FF ** -0.5, 0.109375, ((0, 4),)),
        "down_bias": scatter_about(key_list[11], (D,), 0.3, 2.0, (), jnp.float32),
        "second_gain": jnp.clip(1.0 + 0.18 * jax.random.normal(key_list[12], (D,), jnp.float32), 0.1, 1.9),
        "second_shift": scatter_about(key_list[13], (D,), 0.5, 3.0, (), jnp.float32),
        "lengths": draw_lengths(jax.random.fold_in(key_list[16], 71), 0),
        "cotangent": noise_with(key_list[15], (TOKENS, D), 1.0, 6.0, ((0, 8),), (0, 1, 8, 2.0)),
    }


highest = lax.Precision.HIGHEST
epsilon = 1e-12

@jax.custom_vjp
def low(v):
    return lax.optimization_barrier(v.astype(jnp.bfloat16)).astype(jnp.float32)

@jax.custom_vjp
def low_back(v):
    return v

def low_keep(v):
    return (low(v), None)

def low_pass(kept, grad):
    return (grad,)

def back_keep(v):
    return (v, None)

def back_low(kept, grad):
    return (low(grad),)
low.defvjp(low_keep, low_pass)
low_back.defvjp(back_keep, back_low)

def dense(left, right):
    return jnp.dot(left, right, precision=highest, preferred_element_type=jnp.float32)

def normalize(value, gain, shift):
    centre = value - lax.optimization_barrier(jnp.mean(value, axis=1, keepdims=True))
    scale = lax.rsqrt(lax.optimization_barrier(jnp.mean(centre * centre, axis=1, keepdims=True)) + epsilon)
    return centre * scale * gain + shift

def attend_block(piece, keys_all, values_all, segment_all):
    queries, segment_rows = piece
    raw = jnp.einsum('qhd,khd->hqk', queries, keys_all, precision=highest, preferred_element_type=jnp.float32) * HEAD_DIM ** (-0.5)
    raw = low_back(raw)
    same = segment_rows[:, None] == segment_all[None, :]
    masked = jnp.where(same[None], raw, -1e+30)
    row_max = lax.optimization_barrier(jnp.max(masked, axis=2, keepdims=True))
    exponent = jnp.exp(masked - row_max)
    weights = exponent / lax.optimization_barrier(jnp.sum(exponent, axis=2, keepdims=True))
    return jnp.einsum('hqk,khd->qhd', low(weights), values_all, precision=highest, preferred_element_type=jnp.float32)

def attend_group(piece):
    queries, keys_all, values_all, segment_all = piece
    block_rows = min(512, TOK_DEV)
    block_count = TOK_DEV // block_rows
    blocked = queries.reshape(block_count, block_rows, HEADS, HEAD_DIM)
    segment_blocks = segment_all.reshape(block_count, block_rows)

    def worker(item):
        return attend_block(item, keys_all, values_all, segment_all)
    mixed = lax.map(jax.checkpoint(worker), (blocked, segment_blocks))
    return mixed.reshape(TOK_DEV, HEADS * HEAD_DIM)

def shard_product(left, right):
    columns = left.shape[1] // N_TENSOR
    total = low(dense(left[:, :columns], right[:columns]))
    for shard in range(1, N_TENSOR):
        total = total + low(dense(left[:, shard * columns:(shard + 1) * columns], right[shard * columns:(shard + 1) * columns]))
    return total

def layer(tokens, projections, query_bias, value_bias, mixer, mixer_bias, first_gain, first_shift, up_weight, up_bias, down_weight, down_bias, second_gain, second_shift, segments):
    queries = low_back(low(dense(tokens, projections[0]) + query_bias))
    keys_all = low_back(low(dense(tokens, projections[1])))
    values_all = low_back(low(dense(tokens, projections[2]) + value_bias))
    shaped = (N_DP, TOK_DEV, HEADS, HEAD_DIM)
    mixed = lax.map(attend_group, (queries.reshape(shaped), keys_all.reshape(shaped), values_all.reshape(shaped), segments))
    mixed = low_back(low(mixed.reshape(TOKENS, D)))
    attention = low_back(shard_product(mixed, mixer)) + mixer_bias
    first = normalize(tokens + attention, first_gain, first_shift)
    hidden = low_back(dense(low(first), up_weight) + up_bias)
    active = low(jax.nn.gelu(hidden, approximate=False))
    branch = low_back(shard_product(active, down_weight)) + down_bias
    return normalize(first + branch, second_gain, second_shift)

def reference(tokens, projections, query_bias, value_bias, mixer, mixer_bias, first_gain, first_shift, up_weight, up_bias, down_weight, down_bias, second_gain, second_shift, lengths, cotangent):
    table = lengths.reshape(N_DP, SLOTS).astype(jnp.int32)
    ends = jnp.cumsum(table, axis=1).astype(jnp.int32)
    places = jnp.arange(TOK_DEV, dtype=jnp.int32)
    segments = lax.optimization_barrier(jnp.sum((places[None, :, None] >= ends[:, None, :]).astype(jnp.int32), axis=2)).astype(jnp.int32)
    living = (places[None, :] < ends[:, -1:]).astype(jnp.float32).reshape(TOKENS)
    floats = [array.astype(jnp.float32) for array in (tokens, projections, query_bias, value_bias, mixer, mixer_bias, first_gain, first_shift, up_weight, up_bias, down_weight, down_bias, second_gain, second_shift)]

    def forward(*weights):
        return layer(*weights, segments)
    result, pull = jax.vjp(forward, *floats)
    gradients = pull(cotangent.astype(jnp.float32) * living[:, None])
    return (result.astype(jnp.bfloat16), gradients[0], gradients[1], gradients[2], gradients[3], gradients[4], gradients[5], gradients[6], gradients[7], gradients[8], gradients[9], gradients[10], gradients[11], gradients[12], gradients[13])
```

```python
from functools import partial

import jax
import jax.numpy as jnp
from jax import lax
from jax.experimental import pallas as pl
from jax.experimental.pallas import tpu as pltpu
from jax.sharding import Mesh
from jax.sharding import PartitionSpec as P

HEAD_DIM = 64
LANES = 128
FACTOR = HEAD_DIM ** (-0.5)
epsilon = 1e-12
VMEM_BYTES = 48 * 1024 * 1024
f32 = jnp.float32
bf16 = jnp.bfloat16


def normalize(value):
    centre = value - jnp.mean(value, axis=1, keepdims=True)
    scale = lax.rsqrt(jnp.mean(centre * centre, axis=1, keepdims=True) + epsilon)
    return (centre * scale, scale)


def norm_back(incoming, normed, scale, gain):
    pushed = incoming * gain
    return scale * (
        pushed
        - jnp.mean(pushed, axis=1, keepdims=True)
        - normed * jnp.mean(pushed * normed, axis=1, keepdims=True)
    )


def dot(left, right):
    return jnp.dot(left, right, preferred_element_type=f32)


def contract_rows(left, right):
    return lax.dot_general(left, right, (((0,), (0,)), ((), ())), preferred_element_type=f32)


def contract_cols(left, right):
    return lax.dot_general(left, right, (((1,), (1,)), ((), ())), preferred_element_type=f32)


def three_parts(value):
    high = value.astype(bf16).astype(f32)
    rest = value - high
    middle = rest.astype(bf16).astype(f32)
    return high, middle, rest - middle


def prepare_kernel(lengths_ref, tokens_ref, weight_ref, bias_ref, q_ref, k_ref, kt_ref, v_ref):
    rows, width = q_ref.shape
    product = dot(tokens_ref[...], weight_ref[...]) + bias_ref[...]
    low = product.astype(bf16).astype(f32)
    place = lax.broadcasted_iota(jnp.int32, (rows, 1), 0) + pl.program_id(0) * rows
    segment = jnp.zeros((rows, 1), jnp.int32)
    end = jnp.int32(0)
    for slot in range(lengths_ref.shape[0]):
        end = end + lengths_ref[slot]
        segment = segment + (place >= end).astype(jnp.int32)
    count = lengths_ref.shape[0] + 1
    lane = lax.broadcasted_iota(jnp.int32, (rows, width), 1) % LANES - HEAD_DIM
    same = lane == segment
    in_mask = (lane >= 0) & (lane < count)
    in_sum = (lane >= count) & (lane < count + 3)
    query = jnp.where(lane < 0, low[:, :width] * FACTOR, jnp.where(same, 1.0, 0.0))
    key = jnp.where(
        lane < 0,
        low[:, width : 2 * width],
        jnp.where(in_mask & jnp.logical_not(same), -1e30, jnp.where(in_sum, 1.0, 0.0)),
    )
    value = jnp.where(
        lane < 0, low[:, 2 * width :], jnp.where((lane >= 0) & (lane < 3), 1.0, 0.0)
    )
    q_ref[...] = query.astype(bf16)
    k_ref[...] = key.astype(bf16)
    kt_ref[...] = key.T.astype(bf16)
    v_ref[...] = value.astype(bf16)


def prepare(lengths, tokens, weight, bias, head_count):
    row_count, features = tokens.shape
    width = head_count * LANES
    tile = row_count // 4
    return pl.pallas_call(
        prepare_kernel,
        grid_spec=pltpu.PrefetchScalarGridSpec(
            num_scalar_prefetch=1,
            grid=(row_count // tile,),
            in_specs=[
                pl.BlockSpec((tile, features), lambda i, s: (i, 0)),
                pl.BlockSpec((features, 3 * width), lambda i, s: (0, 0)),
                pl.BlockSpec((1, 3 * width), lambda i, s: (0, 0)),
            ],
            out_specs=[
                pl.BlockSpec((tile, width), lambda i, s: (i, 0)),
                pl.BlockSpec((tile, width), lambda i, s: (i, 0)),
                pl.BlockSpec((width, tile), lambda i, s: (0, i)),
                pl.BlockSpec((tile, width), lambda i, s: (i, 0)),
            ],
        ),
        out_shape=[
            jax.ShapeDtypeStruct((row_count, width), bf16),
            jax.ShapeDtypeStruct((row_count, width), bf16),
            jax.ShapeDtypeStruct((width, row_count), bf16),
            jax.ShapeDtypeStruct((row_count, width), bf16),
        ],
        compiler_params=pltpu.CompilerParams(vmem_limit_bytes=VMEM_BYTES),
        cost_estimate=pl.CostEstimate(
            flops=2 * row_count * features * 3 * width,
            bytes_accessed=8 * row_count * features,
            transcendentals=0,
        ),
        name="prepare",
    )(lengths, tokens, weight, bias)


def forward_kernel(slots, start_ref, q_ref, kt_ref, v_ref, out_ref, kept_ref):
    rows, width = q_ref.shape
    heads = width // LANES
    lane = lax.broadcasted_iota(jnp.int32, (rows, LANES), 1) - HEAD_DIM - slots - 1
    for head in range(heads):
        part = slice(head * LANES, (head + 1) * LANES)
        query = q_ref[:, part]
        scores = dot(query, kt_ref[part, :])
        top = jnp.max(scores, axis=1, keepdims=True)
        weights = jnp.exp(scores - top).astype(bf16)
        mixed = dot(weights, v_ref[:, part])
        total = mixed[:, HEAD_DIM : HEAD_DIM + 1]
        out_ref[:, head * HEAD_DIM : (head + 1) * HEAD_DIM] = (
            mixed[:, :HEAD_DIM] / total
        ).astype(bf16)
        high, middle, low = three_parts(-(top + jnp.log(total)))
        extra = jnp.where(
            lane == 0, high, jnp.where(lane == 1, middle, jnp.where(lane == 2, low, 0.0))
        )
        kept_ref[:, part] = query + extra.astype(bf16)


def attend_forward(start, query, key_t, value, slots, rows):
    row_count, width = query.shape
    heads = width // LANES
    tile = 256
    steps = rows // tile
    return pl.pallas_call(
        partial(forward_kernel, slots),
        grid_spec=pltpu.PrefetchScalarGridSpec(
            num_scalar_prefetch=1,
            grid=(steps,),
            in_specs=[
                pl.BlockSpec((tile, width), lambda i, s: (s[0] * steps + i, 0)),
                pl.BlockSpec((width, row_count), lambda i, s: (0, 0)),
                pl.BlockSpec((row_count, width), lambda i, s: (0, 0)),
            ],
            out_specs=[
                pl.BlockSpec((tile, heads * HEAD_DIM), lambda i, s: (i, 0)),
                pl.BlockSpec((tile, width), lambda i, s: (i, 0)),
            ],
        ),
        out_shape=[
            jax.ShapeDtypeStruct((rows, heads * HEAD_DIM), bf16),
            jax.ShapeDtypeStruct((rows, width), bf16),
        ],
        compiler_params=pltpu.CompilerParams(vmem_limit_bytes=VMEM_BYTES),
        cost_estimate=pl.CostEstimate(
            flops=4 * rows * row_count * width * 2,
            bytes_accessed=4 * row_count * width,
            transcendentals=rows * row_count * heads,
        ),
        name="attend_forward",
    )(start, query, key_t, value)


def backward_kernel(
    first, last, q_ref, g_ref, o_ref, k_ref, kt_ref, v_ref, key_in, value_in, dq_ref, dk_ref, dv_ref, qt, gt, gp, dqt, key_sum, value_sum
):
    rows = q_ref.shape[0]
    row_count, width = k_ref.shape
    heads = width // LANES
    tile = 512
    step = pl.program_id(0)

    @pl.when(step == 0)
    def _():
        if first:
            key_sum[...] = jnp.zeros_like(key_sum)
            value_sum[...] = jnp.zeros_like(value_sum)
        else:
            key_sum[...] = key_in[...]
            value_sum[...] = value_in[...]

    lane = lax.broadcasted_iota(jnp.int32, (rows, LANES), 1) - HEAD_DIM
    for head in range(heads):
        part = slice(head * LANES, (head + 1) * LANES)
        narrow = slice(head * HEAD_DIM, (head + 1) * HEAD_DIM)
        back = g_ref[:, narrow].astype(f32)
        mixed = o_ref[:, narrow].astype(f32)
        centre = -jnp.sum(back * mixed, axis=1, keepdims=True)
        high, middle, low = three_parts(centre)
        extra = jnp.where(
            lane == 0, high, jnp.where(lane == 1, middle, jnp.where(lane == 2, low, 0.0))
        )
        padded = jnp.concatenate([back, jnp.zeros_like(back)], axis=1) + extra
        gp[:, part] = padded.astype(bf16)
        gt[part, :] = padded.T.astype(bf16)
        qt[part, :] = q_ref[:, part].astype(f32).T.astype(bf16)
    dqt[...] = jnp.zeros_like(dqt)

    def advance(index, carry):
        at = pl.multiple_of(index * tile, tile)
        for head in range(heads):
            part = slice(head * LANES, (head + 1) * LANES)
            scores = dot(k_ref[pl.ds(at, tile), part], qt[part, :])
            weights = jnp.exp(scores)
            pushed = dot(v_ref[pl.ds(at, tile), part], gt[part, :])
            score_back = (weights * pushed).astype(bf16)
            value_sum[pl.ds(at, tile), part] += dot(weights.astype(bf16), gp[:, part])
            key_sum[pl.ds(at, tile), part] += dot(score_back, q_ref[:, part])
            top = slice(head * LANES, head * LANES + HEAD_DIM)
            narrow = slice(head * HEAD_DIM, (head + 1) * HEAD_DIM)
            dqt[narrow, :] += dot(kt_ref[top, pl.ds(at, tile)], score_back)
        return carry

    lax.fori_loop(0, row_count // tile, advance, 0)
    dq_ref[...] = (dqt[...] * FACTOR).T.astype(bf16)

    @pl.when(step == pl.num_programs(0) - 1)
    def _():
        if last:
            for head in range(heads):
                top = slice(head * LANES, head * LANES + HEAD_DIM)
                narrow = slice(head * HEAD_DIM, (head + 1) * HEAD_DIM)
                dk_ref[:, narrow] = key_sum[:, top].astype(bf16)
                dv_ref[:, narrow] = value_sum[:, top].astype(bf16)
        else:
            dk_ref[...] = key_sum[...]
            dv_ref[...] = value_sum[...]


def attend_backward(query, back, mixed, key, key_t, value, sums, last):
    rows, width = query.shape
    row_count = key.shape[0]
    heads = width // LANES
    narrow = heads * HEAD_DIM
    first = sums is None
    tile = 512
    steps = rows // tile
    whole = lambda i: (0, 0)
    if first:
        sums = (jnp.zeros((8, LANES), f32), jnp.zeros((8, LANES), f32))
    sum_type = jax.ShapeDtypeStruct((row_count, width), f32)
    if last:
        sum_type = jax.ShapeDtypeStruct((row_count, narrow), bf16)
    return pl.pallas_call(
        partial(backward_kernel, first, last),
        grid=(steps,),
        in_specs=[
            pl.BlockSpec((tile, width), lambda i: (i, 0)),
            pl.BlockSpec((tile, narrow), lambda i: (i, 0)),
            pl.BlockSpec((tile, narrow), lambda i: (i, 0)),
            pl.BlockSpec((row_count, width), whole),
            pl.BlockSpec((width, row_count), whole),
            pl.BlockSpec((row_count, width), whole),
            pl.BlockSpec(sums[0].shape, whole),
            pl.BlockSpec(sums[1].shape, whole),
        ],
        out_specs=[
            pl.BlockSpec((tile, narrow), lambda i: (i, 0)),
            pl.BlockSpec(sum_type.shape, whole),
            pl.BlockSpec(sum_type.shape, whole),
        ],
        out_shape=[jax.ShapeDtypeStruct((rows, narrow), bf16), sum_type, sum_type],
        scratch_shapes=[
            pltpu.VMEM((width, tile), bf16),
            pltpu.VMEM((width, tile), bf16),
            pltpu.VMEM((tile, width), bf16),
            pltpu.VMEM((narrow, tile), f32),
            pltpu.VMEM((row_count, width), f32),
            pltpu.VMEM((row_count, width), f32),
        ],
        compiler_params=pltpu.CompilerParams(vmem_limit_bytes=VMEM_BYTES),
        cost_estimate=pl.CostEstimate(
            flops=10 * rows * row_count * width * 2,
            bytes_accessed=12 * row_count * width,
            transcendentals=rows * row_count * heads,
        ),
        name="attend_backward",
    )(query, back, mixed, key, key_t, value, *sums)


def shift(value, by):
    size = lax.axis_size("tensor")
    return lax.ppermute(value, "tensor", [(i, (i + by) % size) for i in range(size)])


def swap(value):
    return lax.ppermute(value, "core", [(0, 1), (1, 0)])


def cross(value, axis, bit):
    size = lax.axis_size(axis)
    return lax.ppermute(value, axis, [(i, i ^ bit) for i in range(size)])


def order(flag, mine, other, axis):
    return jnp.concatenate(
        [jnp.where(flag == 0, mine, other), jnp.where(flag == 0, other, mine)], axis=axis
    )


def bits_of(axis):
    return [1 << place for place in range(lax.axis_size(axis).bit_length() - 1)]


def gather_quad(value, backwards):
    lead, rows, cols = value.shape
    bits = bits_of("quad")
    me = lax.axis_index("quad")
    held = value.reshape((lead,) + (1,) * len(bits) + (rows, cols))
    for bit in bits[::-1] if backwards else bits:
        other = cross(held, "quad", bit)
        axis = len(bits) - bit.bit_length() + 1
        held = order((me // bit) % 2, held, other, axis)
    return held.reshape(lead, -1, cols)


def scatter_quad(value, backwards):
    bits = bits_of("quad")
    me = lax.axis_index("quad")
    rows = value.shape[0] // lax.axis_size("quad")
    held = value.reshape((2,) * len(bits) + (rows,) + value.shape[1:])
    for bit in bits[::-1] if backwards else bits:
        axis = len(bits) - bit.bit_length()
        flag = (me // bit) % 2
        keep = lax.dynamic_slice_in_dim(held, flag, 1, axis)
        send = lax.dynamic_slice_in_dim(held, 1 - flag, 1, axis)
        other = cross(send, "quad", bit)
        held = (keep.astype(f32) + other.astype(f32)).astype(bf16)
    return held.reshape((rows,) + value.shape[1:])


def sum_everywhere(value):
    for axis in ("core", "quad", "tensor"):
        for bit in bits_of(axis):
            value = value + cross(value, axis, bit)
    return value


def exchange(pieces):
    return [pieces[0]] + [shift(piece, k) for k, piece in enumerate(pieces) if k]


def gelu_parts(hidden):
    gate = 0.5 * (1.0 + lax.erf(hidden * 0.7071067811865476))
    slope = gate + hidden * (0.3989422804014327 * jnp.exp(-0.5 * hidden * hidden))
    return hidden * gate, slope


def local(
    tokens,
    projections,
    query_bias,
    value_bias,
    mixer,
    mixer_bias,
    first_gain,
    first_shift,
    up_weight,
    up_bias,
    down_weight,
    down_bias,
    second_gain,
    second_shift,
    lengths,
    cotangent,
):
    row_count, features = tokens.shape
    columns = projections.shape[2]
    heads = columns // HEAD_DIM
    slots = lengths.shape[0]
    shards = lax.axis_size("tensor")
    quads = lax.axis_size("quad")
    per_share = row_count // shards
    mine = lax.axis_index("tensor")
    core = lax.axis_index("core")
    quad = lax.axis_index("quad")
    offset = mine * per_share
    hidden_count = up_weight.shape[1]
    half = hidden_count // 2

    def own(value):
        return lax.dynamic_slice_in_dim(value, offset, per_share, 0)

    mixer_rows = columns // 2
    bias_half = lax.dynamic_slice_in_dim(up_bias, core * half, half, 0)
    high = lax.reduce_precision(bias_half, 8, 7)
    middle = lax.reduce_precision(bias_half - high, 8, 7)
    low = bias_half - high - middle
    bias_rows = jnp.pad(
        jnp.stack([high, middle, low]).astype(bf16), ((0, 13), (0, features - half))
    )
    mixer_half = jnp.concatenate(
        [lax.dynamic_slice_in_dim(mixer, core * mixer_rows, mixer_rows, 0), bias_rows], axis=0
    )
    mixer_pieces = [mixer_half] + [shift(mixer_half, k) for k in range(1, shards)]
    mixer_stack = jnp.stack(mixer_pieces)
    bias_stack = mixer_stack[:, mixer_rows : mixer_rows + 3, :half].astype(f32)
    hidden_bias = (bias_stack[:, 0] + bias_stack[:, 1]) + bias_stack[:, 2]
    mixer_stack = mixer_stack[:, :mixer_rows]
    mixer_full = order(core, mixer_stack, swap(mixer_stack), 1).reshape(-1, features)

    up_half = lax.dynamic_slice_in_dim(up_weight, core * half, half, 1)
    down_half = lax.dynamic_slice_in_dim(down_weight, core * half, half, 0)
    up_rows, down_rows = features // quads, half // quads
    up_slice = lax.dynamic_slice_in_dim(up_half, quad * up_rows, up_rows, 0)
    down_slice = lax.dynamic_slice_in_dim(down_half, quad * down_rows, down_rows, 0)
    bundle = jnp.concatenate([up_slice.reshape(down_rows, -1), down_slice], axis=1)
    bundles = jnp.stack([shift(bundle, k) for k in range(1, shards)])
    split = up_rows * half // down_rows
    up_far = gather_quad(bundles[:, :, :split].reshape(shards - 1, up_rows, half), False)
    down_far = gather_quad(bundles[:, :, split:], True)
    up_all = jnp.concatenate([up_half[None], up_far], axis=0)
    up_all = jnp.transpose(up_all, (1, 0, 2)).reshape(features, shards * half)
    down_all = jnp.concatenate([down_half[None], down_far], axis=0).reshape(-1, features)

    def padded(weight):
        shaped = weight.reshape(weight.shape[:-1] + (heads, HEAD_DIM))
        wide = jnp.pad(shaped, [(0, 0)] * (shaped.ndim - 1) + [(0, LANES - HEAD_DIM)])
        return wide.reshape(weight.shape[:-1] + (heads * LANES,))

    weight_wide = jnp.transpose(padded(projections), (1, 0, 2)).reshape(features, -1)
    bias_wide = jnp.concatenate(
        [padded(query_bias), jnp.zeros((heads * LANES,), f32), padded(value_bias)]
    )[None]
    query, key, key_t, value = prepare(lengths, tokens, weight_wide, bias_wide, heads)
    mixed_out = [None] * shards
    query_kept = [None] * shards
    mixed_in = [None] * shards
    for k in [shards // 2] + [j for j in range(1, shards) if j != shards // 2] + [0]:
        start = ((mine + k) % shards).astype(jnp.int32).reshape(1)
        mixed_out[k], query_kept[k] = attend_forward(start, query, key_t, value, slots, per_share)
        mixed_in[k] = shift(mixed_out[k], k) if k else mixed_out[0]
    mixed = jnp.concatenate(mixed_in, axis=1)

    attention = dot(mixed, mixer_full)
    first_normed, first_scale = normalize(own(tokens).astype(f32) + attention + mixer_bias)
    first = first_normed * first_gain + first_shift
    first_low = first.astype(bf16)
    first_both = jnp.concatenate([first_low, swap(first_low)], axis=0)
    hidden = dot(first_both, up_all) + hidden_bias.reshape(-1)
    active, slope = gelu_parts(hidden)
    active = active.astype(bf16)
    slope = slope.astype(bf16)
    branch_both = dot(active, down_all)
    branch = branch_both[:per_share] + swap(branch_both[per_share:].astype(bf16)).astype(f32)
    second_normed, second_scale = normalize(first + branch + down_bias)
    layer_output = (second_normed * second_gain + second_shift).astype(bf16)

    places = offset + jnp.arange(per_share, dtype=jnp.int32)
    living = (places < jnp.sum(lengths)).astype(f32)
    incoming = own(cotangent).astype(f32) * living[:, None]
    second_back = norm_back(incoming, second_normed, second_scale, second_gain)
    second_low = second_back.astype(bf16)
    second_both = jnp.concatenate([second_low, swap(second_low)], axis=0)
    hidden_back_wide = contract_cols(second_both, down_all) * slope.astype(f32)
    hidden_back = hidden_back_wide.astype(bf16)
    first_part = contract_cols(hidden_back, up_all)
    first_back = (
        second_back
        + first_part[:per_share]
        + swap(first_part[per_share:].astype(bf16)).astype(f32)
    )
    base_back = norm_back(first_back, first_normed, first_scale, first_gain)
    base_low = base_back.astype(bf16)
    mixed_back = contract_cols(base_low, mixer_full).astype(bf16)

    up_part = contract_rows(first_both, hidden_back).astype(bf16)
    down_part = contract_rows(second_both, active).astype(bf16)
    mixer_part = contract_rows(base_low, mixed).astype(bf16)
    mixer_part = mixer_part.reshape(features, shards, 2, mixer_rows)
    mixer_keep = lax.dynamic_slice_in_dim(mixer_part, core, 1, 2)[:, :, 0]
    mixer_send = lax.dynamic_slice_in_dim(mixer_part, 1 - core, 1, 2)[:, :, 0]
    mixer_part = (mixer_keep.astype(f32) + swap(mixer_send).astype(f32)).astype(bf16)
    mixer_wide = -(-mixer_rows // LANES) * LANES
    mixer_part = jnp.pad(mixer_part, ((0, 0), (0, 0), (0, mixer_wide - mixer_rows)))
    other_part = jnp.concatenate(
        [down_part.reshape(features, shards, half), mixer_part], axis=2
    )
    up_part = scatter_quad(up_part.reshape(features, shards, half), False)
    other_part = scatter_quad(other_part, True)
    both = jnp.concatenate([up_part, other_part], axis=2)
    total = both[:, 0].astype(f32)
    for k in range(1, shards):
        total = total + shift(both[:, k], -k).astype(f32)
    share = features // quads // 2
    total = total.reshape(2, share, -1)
    keep = lax.dynamic_index_in_dim(total, core, 0, False)
    send = lax.dynamic_index_in_dim(total, 1 - core, 0, False)
    other = swap(send.astype(bf16)).astype(f32)

    def halves(begin, size):
        return order(core, keep[:, begin : begin + size], other[:, begin : begin + size], 1)

    up_weight_gradient = halves(0, half)
    down_weight_gradient = halves(half, half).T
    mixer_gradient = halves(2 * half, mixer_rows).T

    hidden_sum = jnp.sum(hidden_back.astype(f32), axis=0).reshape(shards, half)
    owner = (mine - jnp.arange(shards)) % shards
    match = (owner[:, None] == jnp.arange(shards)[None, :]).astype(f32)
    placed = jnp.sum(match[:, :, None] * hidden_sum[:, None, :], axis=0)
    which = (jnp.arange(2) == core).astype(f32)
    placed = placed[:, None, :] * which[None, :, None]
    norm_terms = [
        jnp.sum(first_back * first_normed, axis=0),
        jnp.sum(first_back, axis=0),
        jnp.sum(base_back, axis=0),
        jnp.sum(incoming * second_normed, axis=0),
        jnp.sum(incoming, axis=0),
        jnp.sum(second_back, axis=0),
    ]
    small = sum_everywhere(
        jnp.concatenate(norm_terms + [placed.reshape(-1)]).reshape(-1, LANES)
    ).reshape(-1)
    (
        first_gain_gradient,
        first_shift_gradient,
        mixer_bias_gradient,
        second_gain_gradient,
        second_shift_gradient,
        down_bias_gradient,
    ) = [small[i * features : (i + 1) * features] for i in range(6)]
    up_bias_gradient = lax.dynamic_slice_in_dim(
        small, 6 * features + mine * hidden_count, hidden_count, 0
    )

    back_in = [mixed_back[:, :columns]]
    for k in range(1, shards):
        back_in.append(None)
    back_pieces = [mixed_back[:, k * columns : (k + 1) * columns] for k in range(shards)]
    for k in range(1, shards):
        back_in[k] = shift(back_pieces[k], -k)
    far = list(range(1, shards))
    near_dq, key_sum, value_sum = attend_backward(
        query_kept[0], back_in[0], mixed_out[0], key, key_t, value, None, False
    )
    far_dq, key_back, value_back = attend_backward(
        jnp.concatenate([query_kept[k] for k in far]),
        jnp.concatenate([back_in[k] for k in far]),
        jnp.concatenate([mixed_out[k] for k in far]),
        key,
        key_t,
        value,
        (key_sum, value_sum),
        True,
    )
    weight_rows = jnp.transpose(projections, (1, 0, 2)).reshape(features, 3 * columns)
    weight_far = lax.all_gather(
        lax.dynamic_slice_in_dim(weight_rows, core * (features // 2), features // 2, 0),
        "tensor",
        axis=0,
    )
    weight_all = order(core, weight_far, swap(weight_far), 1)
    input_back = base_back
    query_rows = []
    for k in range(shards):
        piece = (
            near_dq if k == 0 else lax.slice_in_dim(far_dq, (k - 1) * per_share, k * per_share)
        )
        query_rows.append(piece)
        at = ((mine + k) % shards) * per_share
        key_piece = lax.dynamic_slice_in_dim(key_back, at, per_share, 0)
        value_piece = lax.dynamic_slice_in_dim(value_back, at, per_share, 0)
        piece = jnp.concatenate([piece, key_piece, value_piece], axis=1)
        if k:
            piece = shift(piece, k)
        weight = lax.dynamic_index_in_dim(weight_all, (mine - k) % shards, 0, False)
        input_back = input_back + contract_cols(piece, weight)

    rows_in_order = jnp.zeros((row_count, columns), bf16)
    for k in range(shards):
        at = ((mine + k) % shards) * per_share
        rows_in_order = lax.dynamic_update_slice_in_dim(rows_in_order, query_rows[k], at, 0)
    stacked = jnp.concatenate([rows_in_order, key_back, value_back], axis=1)
    gradient = contract_rows(tokens, stacked)
    sums = jnp.sum(stacked.astype(f32), axis=0)
    sums_high = lax.reduce_precision(sums, 8, 7)
    extra = jnp.pad(jnp.stack([sums_high, sums - sums_high]), ((0, 14), (0, 0)))
    extra = jnp.broadcast_to(extra, (quads, 2) + extra.shape)
    gradient = jnp.concatenate([gradient.reshape(quads, 2, share, -1), extra], axis=2)
    keep = lax.dynamic_index_in_dim(gradient, core, 1, False)
    send = lax.dynamic_index_in_dim(gradient, 1 - core, 1, False)
    gradient = keep + swap(send.astype(bf16)).astype(f32)
    if quads == 4:
        mine_rows = lax.dynamic_index_in_dim(gradient, quad, 0, False)
        low_rows = gradient.astype(bf16)
        for bit in (1, 2, 3):
            piece = lax.dynamic_index_in_dim(low_rows, quad ^ bit, 0, False)
            mine_rows = mine_rows + cross(piece, "quad", bit).astype(f32)
    else:
        mine_rows = scatter_quad(
            gradient.astype(bf16).reshape(-1, gradient.shape[2]), False
        ).astype(f32)
    projections_gradient = jnp.transpose(
        mine_rows[:share].reshape(share, 3, columns), (1, 0, 2)
    )
    bias_sums = mine_rows[share] + mine_rows[share + 1]
    query_bias_gradient = bias_sums[:columns]
    value_bias_gradient = bias_sums[2 * columns :]
    return (
        layer_output,
        input_back,
        projections_gradient,
        query_bias_gradient,
        value_bias_gradient,
        mixer_gradient,
        mixer_bias_gradient,
        first_gain_gradient,
        first_shift_gradient,
        up_weight_gradient,
        up_bias_gradient,
        down_weight_gradient,
        down_bias_gradient,
        second_gain_gradient,
        second_shift_gradient,
    )


def solution(mesh):
    dp, tensor = mesh.shape["dp"], mesh.shape["tensor"]
    inner = Mesh(mesh.devices.reshape(dp // 2, 2, tensor), ("quad", "core", "tensor"))
    rows = ("quad", "core")
    in_specs = (
        P(rows, None),
        P(None, None, "tensor"),
        P("tensor"),
        P("tensor"),
        P("tensor", None),
        P(),
        P(),
        P(),
        P(None, "tensor"),
        P("tensor"),
        P("tensor", None),
        P(),
        P(),
        P(),
        P(rows),
        P(rows, None),
    )
    out_specs = (
        P(("quad", "core", "tensor"), None),
        P(("quad", "core", "tensor"), None),
        P(None, rows, "tensor"),
        P("tensor"),
        P("tensor"),
        P("tensor", rows),
        P(),
        P(),
        P(),
        P(rows, "tensor"),
        P("tensor"),
        P("tensor", rows),
        P(),
        P(),
        P(),
    )
    return jax.shard_map(local, mesh=inner, in_specs=in_specs, out_specs=out_specs, check_vma=False)
```

```python
from functools import partial

import jax
import jax.numpy as jnp
from jax import lax
from jax.experimental import pallas as pl
from jax.experimental.pallas import tpu as pltpu
from jax.sharding import Mesh
from jax.sharding import PartitionSpec as P

HEAD_DIM = 64
LANES = 128
FACTOR = HEAD_DIM ** (-0.5)
epsilon = 1e-12
VMEM_BYTES = 32 * 1024 * 1024
WORK_SCALE = 0.2
f32 = jnp.float32
bf16 = jnp.bfloat16


def normalize(value):
    centre = value - jnp.mean(value, axis=1, keepdims=True)
    scale = lax.rsqrt(jnp.mean(centre * centre, axis=1, keepdims=True) + epsilon)
    return (centre * scale, scale)


def norm_back(incoming, normed, scale, gain):
    pushed = incoming * gain
    return scale * (
        pushed
        - jnp.mean(pushed, axis=1, keepdims=True)
        - normed * jnp.mean(pushed * normed, axis=1, keepdims=True)
    )


def dot(left, right):
    return jnp.dot(left, right, preferred_element_type=f32)


def contract_rows(left, right):
    return lax.dot_general(left, right, (((0,), (0,)), ((), ())), preferred_element_type=f32)


def contract_cols(left, right):
    return lax.dot_general(left, right, (((1,), (1,)), ((), ())), preferred_element_type=f32)


def work(microseconds):
    return pl.CostEstimate(
        flops=int(microseconds * WORK_SCALE * 1.15e9), bytes_accessed=0, transcendentals=0
    )


def three_parts(value):
    high = value.astype(bf16).astype(f32)
    rest = value - high
    middle = rest.astype(bf16).astype(f32)
    return high, middle, rest - middle


def prepare_kernel(
    scalars_ref, tokens_ref, weight_ref, bias_ref, q_ref, k_ref, kt_ref, v_ref, rolled_ref
):
    rows, width = q_ref.shape
    slots = scalars_ref.shape[0] - 1
    tokens = tokens_ref[...]
    rolled_ref[...] = tokens
    product = dot(tokens, weight_ref[...]) + bias_ref[...]
    part = lax.rem(scalars_ref[slots] + pl.program_id(0), pl.num_programs(0))
    place = lax.broadcasted_iota(jnp.int32, (rows, 1), 0) + part * rows
    segment = jnp.zeros((rows, 1), jnp.int32)
    end = jnp.int32(0)
    for slot in range(slots):
        end = end + scalars_ref[slot]
        segment = segment + (place >= end).astype(jnp.int32)
    count = slots + 1
    lane = lax.broadcasted_iota(jnp.int32, (rows, LANES), 1) - HEAD_DIM
    same = lane == segment
    in_mask = (lane >= 0) & (lane < count) & jnp.logical_not(same)
    in_sum = (lane >= count) & (lane < count + 3)
    query_more = jnp.where(same, 1.0, 0.0)
    key_more = jnp.where(in_mask, -1e30, jnp.where(in_sum, 1.0, 0.0))
    value_more = jnp.where((lane >= 0) & (lane < 3), 1.0, 0.0)
    for at in range(0, width, LANES):
        part = slice(at, at + LANES)
        query = jnp.where(lane < 0, product[:, part].astype(bf16).astype(f32) * FACTOR, query_more)
        key = jnp.where(lane < 0, product[:, width + at : width + at + LANES], key_more)
        value = jnp.where(
            lane < 0, product[:, 2 * width + at : 2 * width + at + LANES], value_more
        )
        q_ref[:, part] = query.astype(bf16)
        k_ref[:, part] = key.astype(bf16)
        kt_ref[part, :] = key.T.astype(bf16)
        v_ref[:, part] = value.astype(bf16)


def prepare(scalars, tokens, weight, bias, head_count, shards):
    row_count, features = tokens.shape
    width = head_count * LANES
    tile = row_count // shards
    here = lambda i, s: (i, 0)
    last = scalars.shape[0] - 1
    return pl.pallas_call(
        prepare_kernel,
        grid_spec=pltpu.PrefetchScalarGridSpec(
            num_scalar_prefetch=1,
            grid=(shards,),
            in_specs=[
                pl.BlockSpec((tile, features), lambda i, s: (lax.rem(s[last] + i, shards), 0)),
                pl.BlockSpec((features, 3 * width), lambda i, s: (0, 0)),
                pl.BlockSpec((1, 3 * width), lambda i, s: (0, 0)),
            ],
            out_specs=[
                pl.BlockSpec((tile, width), here),
                pl.BlockSpec((tile, width), here),
                pl.BlockSpec((width, tile), lambda i, s: (0, i)),
                pl.BlockSpec((tile, width), here),
                pl.BlockSpec((tile, features), here),
            ],
        ),
        out_shape=[
            jax.ShapeDtypeStruct((row_count, width), bf16),
            jax.ShapeDtypeStruct((row_count, width), bf16),
            jax.ShapeDtypeStruct((width, row_count), bf16),
            jax.ShapeDtypeStruct((row_count, width), bf16),
            jax.ShapeDtypeStruct((row_count, features), bf16),
        ],
        compiler_params=pltpu.CompilerParams(vmem_limit_bytes=VMEM_BYTES),
        cost_estimate=work(8),
        name="prepare",
    )(scalars, tokens, weight, bias)


def forward_kernel(slots, q_ref, kt_ref, v_ref, out_ref, kept_ref):
    rows, width = q_ref.shape
    heads = width // LANES
    lane = lax.broadcasted_iota(jnp.int32, (rows, LANES), 1) - HEAD_DIM - slots - 1
    for head in range(heads):
        part = slice(head * LANES, (head + 1) * LANES)
        query = q_ref[:, part]
        scores = dot(query, kt_ref[part, :])
        top = jnp.max(scores, axis=1, keepdims=True)
        weights = jnp.exp(scores - top).astype(bf16)
        mixed = dot(weights, v_ref[:, part])
        total = mixed[:, HEAD_DIM : HEAD_DIM + 1]
        out_ref[:, head * HEAD_DIM : (head + 1) * HEAD_DIM] = (
            mixed[:, :HEAD_DIM] / total
        ).astype(bf16)
        high, middle, low = three_parts(-(top + jnp.log(total)))
        extra = jnp.where(
            lane == 0, high, jnp.where(lane == 1, middle, jnp.where(lane == 2, low, 0.0))
        )
        kept_ref[:, part] = query + extra.astype(bf16)


def attend_forward(query, key_t, value, slots, begin, rows):
    row_count, width = query.shape
    heads = width // LANES
    tile = 256
    at = begin // tile
    return pl.pallas_call(
        partial(forward_kernel, slots),
        grid=(rows // tile,),
        in_specs=[
            pl.BlockSpec((tile, width), lambda i: (at + i, 0)),
            pl.BlockSpec((width, row_count), lambda i: (0, 0), pipeline_mode=pl.Buffered(1)),
            pl.BlockSpec((row_count, width), lambda i: (0, 0), pipeline_mode=pl.Buffered(1)),
        ],
        out_specs=[
            pl.BlockSpec((tile, heads * HEAD_DIM), lambda i: (i, 0)),
            pl.BlockSpec((tile, width), lambda i: (i, 0)),
        ],
        out_shape=[
            jax.ShapeDtypeStruct((rows, heads * HEAD_DIM), bf16),
            jax.ShapeDtypeStruct((rows, width), bf16),
        ],
        compiler_params=pltpu.CompilerParams(vmem_limit_bytes=VMEM_BYTES),
        cost_estimate=work(5 * rows // 512),
        name="attend_forward",
    )(query, key_t, value)


def backward_kernel(first, last, q_ref, k_ref, kt_ref, v_ref, *refs):
    if first:
        *g_refs, o_ref, dq_ref, pair_ref, gp, gt, qt, dqt, key_sum, value_sum, g_ref = refs
    elif last:
        gp, gt, qt, before_ref, dq_ref, pair_ref, dqt, key_sum, value_sum = refs
    else:
        gp, gt, qt, before_ref, dq_ref, pair_ref, dqt, key_sum, value_sum = refs
    rows, width = q_ref.shape
    keys = k_ref.shape[0]
    heads = width // LANES
    step = pl.program_id(0)
    if first:
        for place, source in enumerate(g_refs):

            @pl.when(step == place)
            def _():
                g_ref[...] = source[...]

        lane = lax.broadcasted_iota(jnp.int32, (rows, LANES), 1) - HEAD_DIM
        for head in range(heads):
            part = slice(head * LANES, (head + 1) * LANES)
            narrow = slice(head * HEAD_DIM, (head + 1) * HEAD_DIM)
            back = g_ref[:, narrow].astype(f32)
            mixed = o_ref[:, narrow].astype(f32)
            centre = -jnp.sum(back * mixed, axis=1, keepdims=True)
            high, middle, low = three_parts(centre)
            extra = jnp.where(
                lane == 0, high, jnp.where(lane == 1, middle, jnp.where(lane == 2, low, 0.0))
            )
            padded = jnp.concatenate([back, jnp.zeros_like(back)], axis=1) + extra
            gp[:, part] = padded.astype(bf16)
            gt[part, :] = padded.T.astype(bf16)
            qt[part, :] = q_ref[:, part].astype(f32).T.astype(bf16)
        dqt[...] = jnp.zeros_like(dqt)
    else:
        dqt[...] = before_ref[...]

    @pl.when(step == 0)
    def _():
        key_sum[...] = jnp.zeros_like(key_sum)
        value_sum[...] = jnp.zeros_like(value_sum)

    for head in range(heads):
        part = slice(head * LANES, (head + 1) * LANES)
        top = slice(head * LANES, head * LANES + HEAD_DIM)
        narrow = slice(head * HEAD_DIM, (head + 1) * HEAD_DIM)
        scores = dot(k_ref[:, part], qt[part, :])
        weights = jnp.exp(scores)
        pushed = dot(v_ref[:, part], gt[part, :])
        score_back = (weights * pushed).astype(bf16)
        value_sum[:, part] += dot(weights.astype(bf16), gp[:, part])
        key_sum[:, part] += dot(score_back, q_ref[:, part])
        dqt[narrow, :] += dot(kt_ref[top, :], score_back)
    if last:
        dq_ref[...] = (dqt[...] * FACTOR).T.astype(bf16)
    else:
        dq_ref[...] = dqt[...]

    @pl.when(step == pl.num_programs(0) - 1)
    def _():
        for head in range(heads):
            top = slice(head * LANES, head * LANES + HEAD_DIM)
            for at, total in enumerate((key_sum, value_sum)):
                place = (at * heads + head) * HEAD_DIM
                pair_ref[:, place : place + HEAD_DIM] = total[:, top].astype(bf16)


def attend_backward(place, count, query, key, key_t, value, more, last):
    row_count, width = query.shape
    heads = width // LANES
    narrow = heads * HEAD_DIM
    rows = row_count // count
    first = len(more) == count + 1
    down = lambda i: (i, 0)
    along = lambda i: (0, i)
    fixed = lambda i: (place, 0)
    in_specs = [
        pl.BlockSpec((rows, width), down),
        pl.BlockSpec((rows, width), fixed),
        pl.BlockSpec((width, rows), lambda i: (0, place)),
        pl.BlockSpec((rows, width), fixed),
    ]
    if first:
        in_specs += [pl.BlockSpec((rows, narrow), lambda i: (0, 0))] * count
        in_specs += [pl.BlockSpec((rows, narrow), down)]
    else:
        in_specs += [
            pl.BlockSpec((rows, width), down),
            pl.BlockSpec((width, rows), along),
            pl.BlockSpec((width, rows), along),
            pl.BlockSpec((narrow, rows), along),
        ]
    if last:
        out_specs = [pl.BlockSpec((rows, narrow), down)]
        out_shape = [jax.ShapeDtypeStruct((row_count, narrow), bf16)]
    else:
        out_specs = [pl.BlockSpec((narrow, rows), along)]
        out_shape = [jax.ShapeDtypeStruct((narrow, row_count), f32)]
    out_specs.append(pl.BlockSpec((rows, 2 * narrow), lambda i: (0, 0)))
    out_shape.append(jax.ShapeDtypeStruct((rows, 2 * narrow), bf16))
    if first:
        out_specs += [
            pl.BlockSpec((rows, width), down),
            pl.BlockSpec((width, rows), along),
            pl.BlockSpec((width, rows), along),
        ]
        out_shape += [
            jax.ShapeDtypeStruct((row_count, width), bf16),
            jax.ShapeDtypeStruct((width, row_count), bf16),
            jax.ShapeDtypeStruct((width, row_count), bf16),
        ]
    return pl.pallas_call(
        partial(backward_kernel, first, last),
        grid=(count,),
        in_specs=in_specs,
        out_specs=out_specs,
        out_shape=out_shape,
        scratch_shapes=[
            pltpu.VMEM((narrow, rows), f32),
            pltpu.VMEM((rows, width), f32),
            pltpu.VMEM((rows, width), f32),
        ]
        + [pltpu.VMEM((rows, narrow), bf16)] * first,
        compiler_params=pltpu.CompilerParams(vmem_limit_bytes=VMEM_BYTES),
        cost_estimate=work(11),
        name="attend_backward",
    )(query, key, key_t, value, *more)


def gelu_parts(hidden):
    gate = 0.5 * (1.0 + lax.erf(hidden * 0.7071067811865476))
    slope = gate + hidden * (0.3989422804014327 * jnp.exp(-0.5 * hidden * hidden))
    return hidden * gate, slope


def wide_forward_kernel(
    mine_ref, other_ref, up_own, up_far, bias_ref, down_own, down_far, active_ref, slope_ref, out_ref, send_ref
):
    rows = mine_ref.shape[0]
    half = up_own.shape[1]
    totals = [None, None]
    for step in range(bias_ref.shape[0]):
        up = up_own[...] if step == 0 else up_far[step - 1]
        down = down_own[...] if step == 0 else down_far[step - 1]
        for at, x_ref in enumerate((mine_ref, other_ref)):
            hidden = dot(x_ref[...], up) + bias_ref[step]
            active, slope = gelu_parts(hidden)
            active = active.astype(bf16)
            place = (slice(at * rows, (at + 1) * rows), slice(step * half, (step + 1) * half))
            active_ref[place] = active
            slope_ref[place] = slope.astype(bf16)
            part = dot(active, down)
            totals[at] = part if step == 0 else totals[at] + part
    out_ref[...] = totals[0]
    send_ref[...] = totals[1].astype(bf16)


def wide_forward(mine, other, up, bias, down):
    rows, features = mine.shape
    pieces, _, half = bias.shape
    whole = pl.BlockSpec(memory_space=pltpu.VMEM)
    return pl.pallas_call(
        wide_forward_kernel,
        in_specs=[whole] * 7,
        out_specs=[whole] * 4,
        out_shape=[
            jax.ShapeDtypeStruct((2 * rows, pieces * half), bf16),
            jax.ShapeDtypeStruct((2 * rows, pieces * half), bf16),
            jax.ShapeDtypeStruct((rows, features), f32),
            jax.ShapeDtypeStruct((rows, features), bf16),
        ],
        compiler_params=pltpu.CompilerParams(vmem_limit_bytes=VMEM_BYTES),
        cost_estimate=work(14),
        name="wide_forward",
    )(mine, other, *up, bias, *down)


def wide_backward_kernel(
    g_mine, g_other, x_mine, x_other, up_own, up_far, down_own, down_far, active_ref, slope_ref, up_part, down_part, bias_part, out_ref, send_ref, gt, xt, hb
):
    rows = g_mine.shape[0]
    half = up_own.shape[1]
    for at, (g_ref, x_ref) in enumerate(((g_mine, x_mine), (g_other, x_other))):
        place = slice(at * rows, (at + 1) * rows)
        gt[:, place] = g_ref[...].astype(f32).T.astype(bf16)
        xt[:, place] = x_ref[...].astype(f32).T.astype(bf16)
    totals = [None, None]
    for step in range(bias_part.shape[0]):
        up = up_own[...] if step == 0 else up_far[step - 1]
        down = down_own[...] if step == 0 else down_far[step - 1]
        across = slice(step * half, (step + 1) * half)
        sums = 0.0
        for at, g_ref in enumerate((g_mine, g_other)):
            place = slice(at * rows, (at + 1) * rows)
            back = contract_cols(g_ref[...], down) * slope_ref[place, across].astype(f32)
            back = back.astype(bf16)
            hb[place, :] = back
            sums = sums + jnp.sum(back.astype(f32), axis=0, keepdims=True)
            part = contract_cols(back, up)
            totals[at] = part if step == 0 else totals[at] + part
        bias_part[step] = sums
        up_part[:, across] = dot(xt[...], hb[...]).astype(bf16)
        down_part[:, across] = dot(gt[...], active_ref[:, across]).astype(bf16)
    out_ref[...] = totals[0]
    send_ref[...] = totals[1].astype(bf16)


def wide_backward(g_mine, g_other, x_mine, x_other, up, down, active, slope):
    rows, features = g_mine.shape
    half = down[0].shape[0]
    pieces = active.shape[1] // half
    whole = pl.BlockSpec(memory_space=pltpu.VMEM)
    return pl.pallas_call(
        wide_backward_kernel,
        in_specs=[whole] * 10,
        out_specs=[whole] * 5,
        out_shape=[
            jax.ShapeDtypeStruct((features, pieces * half), bf16),
            jax.ShapeDtypeStruct((features, pieces * half), bf16),
            jax.ShapeDtypeStruct((pieces, 1, half), f32),
            jax.ShapeDtypeStruct((rows, features), f32),
            jax.ShapeDtypeStruct((rows, features), bf16),
        ],
        scratch_shapes=[
            pltpu.VMEM((features, 2 * rows), bf16),
            pltpu.VMEM((features, 2 * rows), bf16),
            pltpu.VMEM((2 * rows, half), bf16),
        ],
        compiler_params=pltpu.CompilerParams(vmem_limit_bytes=VMEM_BYTES),
        cost_estimate=work(22),
        name="wide_backward",
    )(g_mine, g_other, x_mine, x_other, *up, *down, active, slope)


def shift(value, by):
    size = lax.axis_size("tensor")
    return lax.ppermute(value, "tensor", [(i, (i + by) % size) for i in range(size)])


def swap(value):
    return lax.ppermute(value, "core", [(0, 1), (1, 0)])


def cross(value, axis, bit):
    size = lax.axis_size(axis)
    return lax.ppermute(value, axis, [(i, i ^ bit) for i in range(size)])


def order(flag, mine, other, axis):
    return jnp.concatenate(
        [jnp.where(flag == 0, mine, other), jnp.where(flag == 0, other, mine)], axis=axis
    )


def after(value, *others):
    return lax.optimization_barrier((value,) + others)[0]


def bits_of(axis):
    return [1 << place for place in range(lax.axis_size(axis).bit_length() - 1)]


def gather_step(held, bit, bits):
    flag = (lax.axis_index("quad") // bit) % 2
    return order(flag, held, cross(held, "quad", bit), len(bits) - bit.bit_length() + 1)


def scatter_cut(held, bit, bits):
    axis = len(bits) - bit.bit_length()
    flag = (lax.axis_index("quad") // bit) % 2
    keep = lax.dynamic_slice_in_dim(held, flag, 1, axis)
    return keep, lax.dynamic_slice_in_dim(held, 1 - flag, 1, axis)


def scatter_step(held, bit, bits):
    keep, send = scatter_cut(held, bit, bits)
    return keep, cross(send, "quad", bit)


def joined(pair):
    keep, other = pair
    return (keep.astype(f32) + other.astype(f32)).astype(bf16)


def sum_along(value, axis):
    size = lax.axis_size(axis)
    if axis == "tensor":
        come = [shift(value, k) for k in range(1, size)]
    elif size <= 4:
        come = [cross(value, axis, k) for k in range(1, size)]
    else:
        for bit in bits_of(axis):
            value = value + cross(value, axis, bit)
        return value
    me = lax.axis_index(axis)
    owners = [(me - k) % size if axis == "tensor" else me ^ k for k in range(size)]
    return sum_in_order([value] + come, owners)


def sum_in_order(terms, owners):
    total = 0.0
    for place in range(len(terms)):
        term = terms[0]
        for owner, other in zip(owners[1:], terms[1:]):
            term = jnp.where(owner == place, other, term)
        total = total + term
    return total


def local(
    tokens,
    projections,
    query_bias,
    value_bias,
    mixer,
    mixer_bias,
    first_gain,
    first_shift,
    up_weight,
    up_bias,
    down_weight,
    down_bias,
    second_gain,
    second_shift,
    lengths,
    cotangent,
):
    row_count, features = tokens.shape
    columns = projections.shape[2]
    heads = columns // HEAD_DIM
    slots = lengths.shape[0]
    shards = lax.axis_size("tensor")
    quads = lax.axis_size("quad")
    per_share = row_count // shards
    mine = lax.axis_index("tensor")
    core = lax.axis_index("core")
    quad = lax.axis_index("quad")
    offset = mine * per_share
    hidden_count = up_weight.shape[1]
    half = hidden_count // 2
    bits = bits_of("quad")
    share = features // quads // 2

    def own(value):
        return lax.dynamic_slice_in_dim(value, offset, per_share, 0)

    up_half = lax.dynamic_slice_in_dim(up_weight, core * half, half, 1)
    down_half = lax.dynamic_slice_in_dim(down_weight, core * half, half, 0)
    up_rows, down_rows = features // quads, half // quads
    up_slice = lax.dynamic_slice_in_dim(up_half, quad * up_rows, up_rows, 0)
    down_slice = lax.dynamic_slice_in_dim(down_half, quad * down_rows, down_rows, 0)
    bundle = jnp.concatenate([up_slice.reshape(down_rows, -1), down_slice], axis=1)
    split = up_rows * half // down_rows
    mixer_rows = columns // 2
    bias_half = lax.dynamic_slice_in_dim(up_bias, core * half, half, 0)
    high = lax.reduce_precision(bias_half, 8, 7)
    middle = lax.reduce_precision(bias_half - high, 8, 7)
    low = bias_half - high - middle
    bias_rows = jnp.pad(
        jnp.stack([high, middle, low]).astype(bf16), ((0, 13), (0, features - half))
    )
    mixer_half = jnp.concatenate(
        [lax.dynamic_slice_in_dim(mixer, core * mixer_rows, mixer_rows, 0), bias_rows], axis=0
    )
    mixer_span = mixer_half.shape[0] // 2
    mixer_wide = jnp.concatenate([mixer_half[:mixer_span], mixer_half[mixer_span:]], axis=1)
    bundle = jnp.concatenate([bundle, mixer_wide], axis=0)
    bundles = [shift(bundle, k) for k in range(1, shards)]
    mixer_pieces = [mixer_half] + [
        jnp.concatenate([b[down_rows:, :features], b[down_rows:, features:]], axis=0)
        for b in bundles
    ]
    bundles = [b[:down_rows] for b in bundles]

    def padded(weight):
        shaped = weight.reshape(weight.shape[:-1] + (heads, HEAD_DIM))
        wide = jnp.pad(shaped, [(0, 0)] * (shaped.ndim - 1) + [(0, LANES - HEAD_DIM)])
        return wide.reshape(weight.shape[:-1] + (heads * LANES,))

    weight_wide = jnp.concatenate([padded(projections[i]) for i in range(3)], axis=1)
    bias_wide = jnp.concatenate(
        [padded(query_bias), jnp.zeros((heads * LANES,), f32), padded(value_bias)]
    )[None]
    scalars = jnp.concatenate([lengths, ((mine + 1) % shards).astype(jnp.int32).reshape(1)])
    query, key, key_t, value, rolled = prepare(
        scalars, tokens, weight_wide, bias_wide, heads, shards
    )
    spot = [(k - 1) % shards for k in range(shards)]
    span = row_count // 2
    mixed_first, kept_first = attend_forward(query, key_t, value, slots, 0, span)
    up_far = jnp.stack([b[:, :split].reshape(up_rows, half) for b in bundles])
    down_far = jnp.stack([b[:, split:] for b in bundles])
    ones = (1,) * len(bits)
    up_far = up_far.reshape((shards - 1,) + ones + (up_rows, half))
    down_far = down_far.reshape((shards - 1,) + ones + (down_rows, features))
    query = after(query, up_far, down_far)
    mixed_second, kept_second = attend_forward(query, key_t, value, slots, span, per_share)
    for place, (up_bit, down_bit) in enumerate(zip(bits, bits[::-1])):
        up_far, down_far = gather_step(up_far, up_bit, bits), gather_step(down_far, down_bit, bits)
        if place == 0:
            query = after(query, up_far, down_far)
    mixed_third, kept_third = attend_forward(
        query, key_t, value, slots, span + per_share, per_share
    )
    mixed_pieces = [mixed_first, mixed_second, mixed_third]
    mixed_out = jnp.concatenate(mixed_pieces, axis=0)
    query_kept = jnp.concatenate([kept_first, kept_second, kept_third], axis=0)
    sources = [mixed_first[:per_share], mixed_first[per_share:], mixed_second, mixed_third]
    mixed_in = [shift(sources[spot[k]], k) if k else sources[spot[k]] for k in range(shards)]
    up_all = (up_half, up_far.reshape(-1, features, half))
    down_all = (down_half, down_far.reshape(-1, half, features))
    mixed = jnp.concatenate(mixed_in, axis=1)
    mixer_stack = jnp.stack(mixer_pieces)
    bias_stack = mixer_stack[:, mixer_rows : mixer_rows + 3, :half].astype(f32)
    hidden_bias = (bias_stack[:, 0] + bias_stack[:, 1]) + bias_stack[:, 2]
    mixer_stack = mixer_stack[:, :mixer_rows]
    mixer_full = order(core, mixer_stack, swap(mixer_stack), 1).reshape(-1, features)

    attention = dot(mixed, mixer_full)
    first_normed, first_scale = normalize(own(tokens).astype(f32) + attention + mixer_bias)
    first = first_normed * first_gain + first_shift
    first_low = first.astype(bf16)
    first_other = swap(first_low)
    feature_half = features // 2
    weight_rows = jnp.concatenate([projections[i] for i in range(3)], axis=1)
    weight_own = lax.dynamic_slice_in_dim(weight_rows, core * feature_half, feature_half, 0)
    near = [k for k in range(1, shards) if k != shards // 2]
    weight_list = [weight_own] + [None] * (shards - 1)
    weight_list[near[0]] = shift(after(weight_own, first_low), near[0])
    hidden_bias = after(hidden_bias, weight_list[near[0]])
    active, slope, branch, branch_send = wide_forward(
        first_low, first_other, up_all, hidden_bias[:, None], down_all
    )
    branch = branch + swap(branch_send).astype(f32)
    second_normed, second_scale = normalize(first + branch + down_bias)
    layer_output = (second_normed * second_gain + second_shift).astype(bf16)

    places = offset + jnp.arange(per_share, dtype=jnp.int32)
    living = (places < jnp.sum(lengths)).astype(f32)
    incoming = own(cotangent).astype(f32) * living[:, None]
    second_back = norm_back(incoming, second_normed, second_scale, second_gain)
    second_low = second_back.astype(bf16)
    for k in near[1:]:
        weight_list[k] = shift(after(weight_own, weight_list[near[0]]), k)
        second_low = after(second_low, weight_list[k])
    second_other = swap(second_low)
    up_part, down_part, hidden_sum, first_part, first_send = wide_backward(
        second_low, second_other, first_low, first_other, up_all, down_all, active, slope
    )
    weight_list[shards // 2] = shift(after(weight_own, weight_list[near[-1]]), shards // 2)
    up_part = after(up_part, weight_list[shards // 2])
    blocks = (2,) * len(bits) + (features // quads,)
    up_keep, up_send = scatter_cut(up_part.reshape(blocks + (-1,)), bits[0], bits)
    up_come = cross(up_send, "quad", bits[0])
    first_back = second_back + first_part + swap(first_send).astype(f32)
    base_back = norm_back(first_back, first_normed, first_scale, first_gain)
    base_low = base_back.astype(bf16)
    mixed_back = contract_cols(base_low, mixer_full).astype(bf16)
    back_in = [mixed_back[:, :columns]] + [
        shift(mixed_back[:, k * columns : (k + 1) * columns], -k) for k in range(1, shards)
    ]
    back_all = [back_in[(p + 1) % shards] for p in range(shards)]

    def mixed_half(which):
        begin = [k * columns for k in range(shards)]
        return jnp.concatenate(
            [
                jnp.where(
                    which == 0,
                    mixed[:, at : at + mixer_rows],
                    mixed[:, at + mixer_rows : at + columns],
                )
                for at in begin
            ],
            axis=1,
        )

    mixer_send = contract_rows(base_low, mixed_half(1 - core)).astype(bf16)
    mixer_keep = contract_rows(base_low, mixed_half(core))
    mixer_part = (mixer_keep + swap(mixer_send).astype(f32)).astype(bf16)
    other_part = jnp.concatenate([down_part, mixer_part], axis=1)
    other_keep, other_send = scatter_cut(other_part.reshape(blocks + (-1,)), bits[-1], bits)
    other_come = cross(other_send, "quad", bits[-1])

    owner = (mine - jnp.arange(shards)) % shards
    match = (owner[:, None] == jnp.arange(shards)[None, :]).astype(f32)
    placed = jnp.sum(match[:, :, None] * hidden_sum, axis=0)
    which = (jnp.arange(2) == core).astype(f32)
    placed = placed[:, None, :] * which[None, :, None]
    norm_terms = [
        jnp.sum(first_back * first_normed, axis=0),
        jnp.sum(first_back, axis=0),
        jnp.sum(base_back, axis=0),
        jnp.sum(incoming * second_normed, axis=0),
        jnp.sum(incoming, axis=0),
        jnp.sum(second_back, axis=0),
    ]
    small = jnp.concatenate(norm_terms + [placed.reshape(-1)]).reshape(-1, LANES)

    turns = [k for k in range(1, shards) if k != shards // 2] + [shards // 2, 0]
    pairs = [None] * shards
    come = [None] * shards
    more = (*back_all, after(mixed_out, up_send, other_send))
    for turn, k in enumerate(turns):
        query_now = query_kept
        if turn == 2:
            up_sum = joined((up_keep, up_come))
            keep, send = scatter_cut(up_sum, bits[1], bits)
            query_now = after(query_now, come[turns[0]], send)
            up_sum = (keep, cross(send, "quad", bits[1]))
        if turn == 3:
            other_sum = joined((other_keep, other_come))
            keep, send = scatter_cut(other_sum, bits[-2], bits)
            query_now = after(query_now, come[turns[1]], send)
            other_sum = (keep, cross(send, "quad", bits[-2]))
        query_sum, pairs[k], *kept = attend_backward(
            spot[k], shards, query_now, key, key_t, value, more, turn == shards - 1
        )
        if kept:
            transposed = kept
        more = (*transposed, query_sum)
        come[k] = shift(pairs[k], k) if k else pairs[k]
    query_all = query_sum
    pair_all = jnp.concatenate([pairs[(p + 1) % shards] for p in range(shards)], axis=0)
    for up_bit, other_bit in zip(bits[2:], bits[::-1][2:]):
        up_sum = scatter_step(joined(up_sum), up_bit, bits)
        other_sum = scatter_step(joined(other_sum), other_bit, bits)
    up_sum = joined(up_sum).reshape(features // quads, -1)
    other_sum = joined(other_sum).reshape(features // quads, -1)
    def piece_of(k):
        down_at, mixer_at = k * half, shards * half + k * mixer_rows
        return jnp.concatenate(
            [
                up_sum[:, k * half : (k + 1) * half],
                other_sum[:, down_at : down_at + half],
                other_sum[:, mixer_at : mixer_at + mixer_rows],
            ],
            axis=1,
        )

    total_pieces = [piece_of(k) for k in range(shards)]
    weight_mine = after(jnp.concatenate(weight_list, axis=0), pairs[turns[0]])
    come = [after(piece, query_all) for piece in come]
    weight_other = swap(weight_mine)
    input_halves = []
    query_come = [
        shift(query_all[spot[k] * per_share : (spot[k] + 1) * per_share], k)
        if k
        else query_all[spot[0] * per_share :]
        for k in range(shards)
    ]
    for weight_all in (weight_mine, weight_other):
        total = 0.0
        for k in turns[:-2] + [0, shards // 2]:
            weight = weight_all[k * feature_half : (k + 1) * feature_half]
            total = total + contract_cols(query_come[k], weight[:, :columns])
            total = total + contract_cols(come[k], weight[:, columns:])
        input_halves.append(total)
    input_back = base_back + order(core, input_halves[0], input_halves[1], 1)
    total = total_pieces[0].astype(f32)
    for k in range(1, shards):
        total_come = shift(total_pieces[k], -k)
        if k == 1:
            small = after(small, query_all, total_come)
        total = total + total_come.astype(f32)
    for axis in ("core", "quad", "tensor"):
        small = sum_along(small, axis)
    small = small.reshape(-1)
    total = total.reshape(2, share, -1)
    keep = lax.dynamic_index_in_dim(total, core, 0, False)
    send = lax.dynamic_index_in_dim(total, 1 - core, 0, False)
    other = swap(send.astype(bf16)).astype(f32)

    def halves(begin, size):
        return order(core, keep[:, begin : begin + size], other[:, begin : begin + size], 1)

    up_weight_gradient = halves(0, half)
    down_weight_gradient = halves(half, half).T
    mixer_gradient = halves(2 * half, mixer_rows).T
    (
        first_gain_gradient,
        first_shift_gradient,
        mixer_bias_gradient,
        second_gain_gradient,
        second_shift_gradient,
        down_bias_gradient,
    ) = [small[i * features : (i + 1) * features] for i in range(6)]
    up_bias_gradient = lax.dynamic_slice_in_dim(
        small, 6 * features + mine * hidden_count, hidden_count, 0
    )

    gradient = jnp.concatenate(
        [contract_rows(rolled, query_all), contract_rows(rolled, pair_all)], axis=1
    )
    sums = jnp.concatenate(
        [jnp.sum(query_all.astype(f32), axis=0), jnp.sum(pair_all.astype(f32), axis=0)]
    )

    def split_sum(sums):
        high = lax.reduce_precision(sums, 8, 7)
        return high + lax.reduce_precision(sums - high, 8, 7)

    def with_sums(rows, sums):
        high = lax.reduce_precision(sums, 8, 7)
        extra = jnp.pad(jnp.stack([high, sums - high]), ((0, 14), (0, 0)))
        return jnp.concatenate([rows.astype(bf16), extra.astype(bf16)], axis=0)

    gradient = gradient.reshape(quads, 2, share, -1)
    keep = lax.dynamic_index_in_dim(gradient, core, 1, False).reshape(quads * share, -1)
    send = lax.dynamic_index_in_dim(gradient, 1 - core, 1, False).reshape(quads * share, -1)
    other = swap(with_sums(send, sums)).astype(f32)
    gradient = keep + other[:-16]
    sums = split_sum(sums) + (other[-16] + other[-15])
    if quads <= 4:
        pieces = [lax.dynamic_slice_in_dim(gradient, (quad ^ k) * share, share, 0) for k in range(quads)]
        come = [cross(with_sums(pieces[k], sums), "quad", k).astype(f32) for k in range(1, quads)]
        gradient = pieces[0] + sum(piece[:-16] for piece in come)
        sums = sum_in_order(
            [split_sum(sums)] + [piece[-16] + piece[-15] for piece in come],
            [quad ^ k for k in range(quads)],
        )
    else:
        low_rows = jnp.concatenate(
            [with_sums(gradient[q * share : (q + 1) * share], sums) for q in range(quads)]
        ).reshape((2,) * len(bits) + (share + 16, -1))
        for bit in bits:
            low_rows = joined(scatter_step(low_rows, bit, bits))
        low_rows = low_rows.reshape(share + 16, -1).astype(f32)
        gradient = low_rows[:share]
        sums = low_rows[share] + low_rows[share + 1]
    projections_gradient = jnp.stack(
        [gradient[:, i * columns : (i + 1) * columns] for i in range(3)]
    )
    query_bias_gradient = sums[:columns]
    value_bias_gradient = sums[2 * columns :]
    return (
        layer_output,
        input_back,
        projections_gradient,
        query_bias_gradient,
        value_bias_gradient,
        mixer_gradient,
        mixer_bias_gradient,
        first_gain_gradient,
        first_shift_gradient,
        up_weight_gradient,
        up_bias_gradient,
        down_weight_gradient,
        down_bias_gradient,
        second_gain_gradient,
        second_shift_gradient,
    )


def solution(mesh):
    dp, tensor = mesh.shape["dp"], mesh.shape["tensor"]
    inner = Mesh(mesh.devices.reshape(dp // 2, 2, tensor), ("quad", "core", "tensor"))
    rows = ("quad", "core")
    in_specs = (
        P(rows, None),
        P(None, None, "tensor"),
        P("tensor"),
        P("tensor"),
        P("tensor", None),
        P(),
        P(),
        P(),
        P(None, "tensor"),
        P("tensor"),
        P("tensor", None),
        P(),
        P(),
        P(),
        P(rows),
        P(rows, None),
    )
    out_specs = (
        P(("quad", "core", "tensor"), None),
        P(("quad", "core", "tensor"), None),
        P(None, rows, "tensor"),
        P("tensor"),
        P("tensor"),
        P("tensor", rows),
        P(),
        P(),
        P(),
        P(rows, "tensor"),
        P("tensor"),
        P("tensor", rows),
        P(),
        P(),
        P(),
    )
    return jax.shard_map(local, mesh=inner, in_specs=in_specs, out_specs=out_specs, check_vma=False)
```

```python
from functools import partial

import jax
import jax.numpy as jnp
from jax import lax
from jax.experimental import pallas as pl
from jax.experimental.pallas import tpu as pltpu
from jax.sharding import Mesh
from jax.sharding import PartitionSpec as P

HEAD_DIM = 64
LANES = 128
FACTOR = HEAD_DIM ** (-0.5)
epsilon = 1e-12
VMEM_BYTES = 32 * 1024 * 1024
WORK_SCALE = 1.0
f32 = jnp.float32
bf16 = jnp.bfloat16


def normalize(value):
    centre = value - jnp.mean(value, axis=1, keepdims=True)
    scale = lax.rsqrt(jnp.mean(centre * centre, axis=1, keepdims=True) + epsilon)
    return (centre * scale, scale)


def norm_back(incoming, normed, scale, gain):
    pushed = incoming * gain
    return scale * (
        pushed
        - jnp.mean(pushed, axis=1, keepdims=True)
        - normed * jnp.mean(pushed * normed, axis=1, keepdims=True)
    )


def dot(left, right):
    return jnp.dot(left, right, preferred_element_type=f32)


def contract_rows(left, right):
    return lax.dot_general(left, right, (((0,), (0,)), ((), ())), preferred_element_type=f32)


def contract_cols(left, right):
    return lax.dot_general(left, right, (((1,), (1,)), ((), ())), preferred_element_type=f32)


def work(microseconds):
    return pl.CostEstimate(
        flops=int(microseconds * WORK_SCALE * 1.15e9), bytes_accessed=0, transcendentals=0
    )


def three_parts(value):
    high = value.astype(bf16).astype(f32)
    rest = value - high
    middle = rest.astype(bf16).astype(f32)
    return high, middle, rest - middle


def prepare_kernel(
    scalars_ref, tokens_ref, weight_ref, bias_ref, q_ref, k_ref, kt_ref, v_ref, rolled_ref
):
    rows, width = q_ref.shape
    slots = scalars_ref.shape[0] - 1
    tokens = tokens_ref[...]
    rolled_ref[...] = tokens
    product = dot(tokens, weight_ref[...]) + bias_ref[...]
    part = lax.rem(scalars_ref[slots] + pl.program_id(0), pl.num_programs(0))
    place = lax.broadcasted_iota(jnp.int32, (rows, 1), 0) + part * rows
    segment = jnp.zeros((rows, 1), jnp.int32)
    end = jnp.int32(0)
    for slot in range(slots):
        end = end + scalars_ref[slot]
        segment = segment + (place >= end).astype(jnp.int32)
    count = slots + 1
    lane = lax.broadcasted_iota(jnp.int32, (rows, LANES), 1) - HEAD_DIM
    same = lane == segment
    in_mask = (lane >= 0) & (lane < count) & jnp.logical_not(same)
    in_sum = (lane >= count) & (lane < count + 3)
    query_more = jnp.where(same, 1.0, 0.0)
    key_more = jnp.where(in_mask, -1e30, jnp.where(in_sum, 1.0, 0.0))
    value_more = jnp.where((lane >= 0) & (lane < 3), 1.0, 0.0)
    for at in range(0, width, LANES):
        part = slice(at, at + LANES)
        query = jnp.where(lane < 0, product[:, part].astype(bf16).astype(f32) * FACTOR, query_more)
        key = jnp.where(lane < 0, product[:, width + at : width + at + LANES], key_more)
        value = jnp.where(
            lane < 0, product[:, 2 * width + at : 2 * width + at + LANES], value_more
        )
        q_ref[:, part] = query.astype(bf16)
        k_ref[:, part] = key.astype(bf16)
        kt_ref[part, :] = key.T.astype(bf16)
        v_ref[:, part] = value.astype(bf16)


def prepare(scalars, tokens, weight, bias, head_count, shards):
    row_count, features = tokens.shape
    width = head_count * LANES
    tile = row_count // shards
    here = lambda i, s: (i, 0)
    last = scalars.shape[0] - 1
    return pl.pallas_call(
        prepare_kernel,
        grid_spec=pltpu.PrefetchScalarGridSpec(
            num_scalar_prefetch=1,
            grid=(shards,),
            in_specs=[
                pl.BlockSpec((tile, features), lambda i, s: (lax.rem(s[last] + i, shards), 0)),
                pl.BlockSpec((features, 3 * width), lambda i, s: (0, 0)),
                pl.BlockSpec((1, 3 * width), lambda i, s: (0, 0)),
            ],
            out_specs=[
                pl.BlockSpec((tile, width), here),
                pl.BlockSpec((tile, width), here),
                pl.BlockSpec((width, tile), lambda i, s: (0, i)),
                pl.BlockSpec((tile, width), here),
                pl.BlockSpec((tile, features), here),
            ],
        ),
        out_shape=[
            jax.ShapeDtypeStruct((row_count, width), bf16),
            jax.ShapeDtypeStruct((row_count, width), bf16),
            jax.ShapeDtypeStruct((width, row_count), bf16),
            jax.ShapeDtypeStruct((row_count, width), bf16),
            jax.ShapeDtypeStruct((row_count, features), bf16),
        ],
        compiler_params=pltpu.CompilerParams(vmem_limit_bytes=VMEM_BYTES),
        cost_estimate=work(8),
        name="prepare",
    )(scalars, tokens, weight, bias)


def forward_kernel(slots, q_ref, kt_ref, v_ref, out_ref, kept_ref):
    rows, width = q_ref.shape
    heads = width // LANES
    lane = lax.broadcasted_iota(jnp.int32, (rows, LANES), 1) - HEAD_DIM - slots - 1
    for head in range(heads):
        part = slice(head * LANES, (head + 1) * LANES)
        query = q_ref[:, part]
        scores = dot(query, kt_ref[part, :])
        top = jnp.max(scores, axis=1, keepdims=True)
        weights = jnp.exp(scores - top).astype(bf16)
        mixed = dot(weights, v_ref[:, part])
        total = mixed[:, HEAD_DIM : HEAD_DIM + 1]
        out_ref[:, head * HEAD_DIM : (head + 1) * HEAD_DIM] = (
            mixed[:, :HEAD_DIM] / total
        ).astype(bf16)
        high, middle, low = three_parts(-(top + jnp.log(total)))
        extra = jnp.where(
            lane == 0, high, jnp.where(lane == 1, middle, jnp.where(lane == 2, low, 0.0))
        )
        kept_ref[:, part] = query + extra.astype(bf16)


def attend_forward(query, key_t, value, slots, begin, rows):
    row_count, width = query.shape
    heads = width // LANES
    tile = 256
    at = begin // tile
    return pl.pallas_call(
        partial(forward_kernel, slots),
        grid=(rows // tile,),
        in_specs=[
            pl.BlockSpec((tile, width), lambda i: (at + i, 0)),
            pl.BlockSpec((width, row_count), lambda i: (0, 0), pipeline_mode=pl.Buffered(1)),
            pl.BlockSpec((row_count, width), lambda i: (0, 0), pipeline_mode=pl.Buffered(1)),
        ],
        out_specs=[
            pl.BlockSpec((tile, heads * HEAD_DIM), lambda i: (i, 0)),
            pl.BlockSpec((tile, width), lambda i: (i, 0)),
        ],
        out_shape=[
            jax.ShapeDtypeStruct((rows, heads * HEAD_DIM), bf16),
            jax.ShapeDtypeStruct((rows, width), bf16),
        ],
        compiler_params=pltpu.CompilerParams(vmem_limit_bytes=VMEM_BYTES),
        cost_estimate=work(5 * rows // 512),
        name="attend_forward",
    )(query, key_t, value)


def backward_kernel(first, last, q_ref, k_ref, kt_ref, v_ref, *refs):
    if first:
        *g_refs, o_ref, dq_ref, pair_ref, gp, gt, qt, dqt, key_sum, value_sum, g_ref = refs
    elif last:
        gp, gt, qt, before_ref, dq_ref, pair_ref, dqt, key_sum, value_sum = refs
    else:
        gp, gt, qt, before_ref, dq_ref, pair_ref, dqt, key_sum, value_sum = refs
    rows, width = q_ref.shape
    keys = k_ref.shape[0]
    heads = width // LANES
    step = pl.program_id(0)
    if first:
        for place, source in enumerate(g_refs):

            @pl.when(step == place)
            def _():
                g_ref[...] = source[...]

        lane = lax.broadcasted_iota(jnp.int32, (rows, LANES), 1) - HEAD_DIM
        for head in range(heads):
            part = slice(head * LANES, (head + 1) * LANES)
            narrow = slice(head * HEAD_DIM, (head + 1) * HEAD_DIM)
            back = g_ref[:, narrow].astype(f32)
            mixed = o_ref[:, narrow].astype(f32)
            centre = -jnp.sum(back * mixed, axis=1, keepdims=True)
            high, middle, low = three_parts(centre)
            extra = jnp.where(
                lane == 0, high, jnp.where(lane == 1, middle, jnp.where(lane == 2, low, 0.0))
            )
            padded = jnp.concatenate([back, jnp.zeros_like(back)], axis=1) + extra
            gp[:, part] = padded.astype(bf16)
            gt[part, :] = padded.T.astype(bf16)
            qt[part, :] = q_ref[:, part].astype(f32).T.astype(bf16)
        dqt[...] = jnp.zeros_like(dqt)
    else:
        dqt[...] = before_ref[...]

    @pl.when(step == 0)
    def _():
        key_sum[...] = jnp.zeros_like(key_sum)
        value_sum[...] = jnp.zeros_like(value_sum)

    for head in range(heads):
        part = slice(head * LANES, (head + 1) * LANES)
        top = slice(head * LANES, head * LANES + HEAD_DIM)
        narrow = slice(head * HEAD_DIM, (head + 1) * HEAD_DIM)
        scores = dot(k_ref[:, part], qt[part, :])
        weights = jnp.exp(scores)
        pushed = dot(v_ref[:, part], gt[part, :])
        score_back = (weights * pushed).astype(bf16)
        value_sum[:, part] += dot(weights.astype(bf16), gp[:, part])
        key_sum[:, part] += dot(score_back, q_ref[:, part])
        dqt[narrow, :] += dot(kt_ref[top, :], score_back)
    if last:
        dq_ref[...] = (dqt[...] * FACTOR).T.astype(bf16)
    else:
        dq_ref[...] = dqt[...]

    @pl.when(step == pl.num_programs(0) - 1)
    def _():
        for head in range(heads):
            top = slice(head * LANES, head * LANES + HEAD_DIM)
            for at, total in enumerate((key_sum, value_sum)):
                place = (at * heads + head) * HEAD_DIM
                pair_ref[:, place : place + HEAD_DIM] = total[:, top].astype(bf16)


def attend_backward(place, count, query, key, key_t, value, more, last):
    row_count, width = query.shape
    heads = width // LANES
    narrow = heads * HEAD_DIM
    rows = row_count // count
    first = len(more) == count + 1
    down = lambda i: (i, 0)
    along = lambda i: (0, i)
    fixed = lambda i: (place, 0)
    in_specs = [
        pl.BlockSpec((rows, width), down),
        pl.BlockSpec((rows, width), fixed),
        pl.BlockSpec((width, rows), lambda i: (0, place)),
        pl.BlockSpec((rows, width), fixed),
    ]
    if first:
        in_specs += [pl.BlockSpec((rows, narrow), lambda i: (0, 0))] * count
        in_specs += [pl.BlockSpec((rows, narrow), down)]
    else:
        in_specs += [
            pl.BlockSpec((rows, width), down),
            pl.BlockSpec((width, rows), along),
            pl.BlockSpec((width, rows), along),
            pl.BlockSpec((narrow, rows), along),
        ]
    if last:
        out_specs = [pl.BlockSpec((rows, narrow), down)]
        out_shape = [jax.ShapeDtypeStruct((row_count, narrow), bf16)]
    else:
        out_specs = [pl.BlockSpec((narrow, rows), along)]
        out_shape = [jax.ShapeDtypeStruct((narrow, row_count), f32)]
    out_specs.append(pl.BlockSpec((rows, 2 * narrow), lambda i: (0, 0)))
    out_shape.append(jax.ShapeDtypeStruct((rows, 2 * narrow), bf16))
    if first:
        out_specs += [
            pl.BlockSpec((rows, width), down),
            pl.BlockSpec((width, rows), along),
            pl.BlockSpec((width, rows), along),
        ]
        out_shape += [
            jax.ShapeDtypeStruct((row_count, width), bf16),
            jax.ShapeDtypeStruct((width, row_count), bf16),
            jax.ShapeDtypeStruct((width, row_count), bf16),
        ]
    return pl.pallas_call(
        partial(backward_kernel, first, last),
        grid=(count,),
        in_specs=in_specs,
        out_specs=out_specs,
        out_shape=out_shape,
        scratch_shapes=[
            pltpu.VMEM((narrow, rows), f32),
            pltpu.VMEM((rows, width), f32),
            pltpu.VMEM((rows, width), f32),
        ]
        + [pltpu.VMEM((rows, narrow), bf16)] * first,
        compiler_params=pltpu.CompilerParams(vmem_limit_bytes=VMEM_BYTES),
        cost_estimate=work(11),
        name="attend_backward",
    )(query, key, key_t, value, *more)


def gelu_parts(hidden):
    gate = 0.5 * (1.0 + lax.erf(hidden * 0.7071067811865476))
    slope = gate + hidden * (0.3989422804014327 * jnp.exp(-0.5 * hidden * hidden))
    return hidden * gate, slope


def wide_forward_kernel(
    mine_ref, other_ref, up_own, up_far, bias_ref, down_own, down_far, active_ref, slope_ref, out_ref, send_ref
):
    rows = mine_ref.shape[0]
    half = up_own.shape[1]
    totals = [None, None]
    for step in range(bias_ref.shape[0]):
        up = up_own[...] if step == 0 else up_far[step - 1]
        down = down_own[...] if step == 0 else down_far[step - 1]
        for at, x_ref in enumerate((mine_ref, other_ref)):
            hidden = dot(x_ref[...], up) + bias_ref[step]
            active, slope = gelu_parts(hidden)
            active = active.astype(bf16)
            place = (slice(at * rows, (at + 1) * rows), slice(step * half, (step + 1) * half))
            active_ref[place] = active
            slope_ref[place] = slope.astype(bf16)
            part = dot(active, down)
            totals[at] = part if step == 0 else totals[at] + part
    out_ref[...] = totals[0]
    send_ref[...] = totals[1].astype(bf16)


def wide_forward(mine, other, up, bias, down):
    rows, features = mine.shape
    pieces, _, half = bias.shape
    whole = pl.BlockSpec(memory_space=pltpu.VMEM)
    return pl.pallas_call(
        wide_forward_kernel,
        in_specs=[whole] * 7,
        out_specs=[whole] * 4,
        out_shape=[
            jax.ShapeDtypeStruct((2 * rows, pieces * half), bf16),
            jax.ShapeDtypeStruct((2 * rows, pieces * half), bf16),
            jax.ShapeDtypeStruct((rows, features), f32),
            jax.ShapeDtypeStruct((rows, features), bf16),
        ],
        compiler_params=pltpu.CompilerParams(vmem_limit_bytes=VMEM_BYTES),
        cost_estimate=work(14),
        name="wide_forward",
    )(mine, other, *up, bias, *down)


def wide_backward_kernel(
    g_mine, g_other, x_mine, x_other, up_own, up_far, down_own, down_far, active_ref, slope_ref, up_part, down_part, bias_part, out_ref, send_ref, gt, xt, hb
):
    rows = g_mine.shape[0]
    half = up_own.shape[1]
    for at, (g_ref, x_ref) in enumerate(((g_mine, x_mine), (g_other, x_other))):
        place = slice(at * rows, (at + 1) * rows)
        gt[:, place] = g_ref[...].astype(f32).T.astype(bf16)
        xt[:, place] = x_ref[...].astype(f32).T.astype(bf16)
    totals = [None, None]
    for step in range(bias_part.shape[0]):
        up = up_own[...] if step == 0 else up_far[step - 1]
        down = down_own[...] if step == 0 else down_far[step - 1]
        across = slice(step * half, (step + 1) * half)
        sums = 0.0
        for at, g_ref in enumerate((g_mine, g_other)):
            place = slice(at * rows, (at + 1) * rows)
            back = contract_cols(g_ref[...], down) * slope_ref[place, across].astype(f32)
            back = back.astype(bf16)
            hb[place, :] = back
            sums = sums + jnp.sum(back.astype(f32), axis=0, keepdims=True)
            part = contract_cols(back, up)
            totals[at] = part if step == 0 else totals[at] + part
        bias_part[step] = sums
        up_part[:, across] = dot(xt[...], hb[...]).astype(bf16)
        down_part[:, across] = dot(gt[...], active_ref[:, across]).astype(bf16)
    out_ref[...] = totals[0]
    send_ref[...] = totals[1].astype(bf16)


def wide_backward(g_mine, g_other, x_mine, x_other, up, down, active, slope):
    rows, features = g_mine.shape
    half = down[0].shape[0]
    pieces = active.shape[1] // half
    whole = pl.BlockSpec(memory_space=pltpu.VMEM)
    return pl.pallas_call(
        wide_backward_kernel,
        in_specs=[whole] * 10,
        out_specs=[whole] * 5,
        out_shape=[
            jax.ShapeDtypeStruct((features, pieces * half), bf16),
            jax.ShapeDtypeStruct((features, pieces * half), bf16),
            jax.ShapeDtypeStruct((pieces, 1, half), f32),
            jax.ShapeDtypeStruct((rows, features), f32),
            jax.ShapeDtypeStruct((rows, features), bf16),
        ],
        scratch_shapes=[
            pltpu.VMEM((features, 2 * rows), bf16),
            pltpu.VMEM((features, 2 * rows), bf16),
            pltpu.VMEM((2 * rows, half), bf16),
        ],
        compiler_params=pltpu.CompilerParams(vmem_limit_bytes=VMEM_BYTES),
        cost_estimate=work(22),
        name="wide_backward",
    )(g_mine, g_other, x_mine, x_other, *up, *down, active, slope)


def collect_kernel(scalars_ref, *refs):
    *norm_refs, hidden_ref, out_ref, rows_ref = refs
    half = out_ref.shape[1]
    count = out_ref.shape[0] // 2
    shards = hidden_ref.shape[0]
    rows_ref[...] = jnp.zeros_like(rows_ref)
    for at, ref in enumerate(norm_refs):
        for side in range(2):
            rows_ref[2 * at + side : 2 * at + side + 1, :] = ref[:, side * half : (side + 1) * half]
    line = lax.broadcasted_iota(jnp.int32, (count, half), 0) - 2 * len(norm_refs)
    total = rows_ref[...]
    for piece in range(shards):
        owner = lax.rem(scalars_ref[0] - piece + shards, shards)
        total = jnp.where(line == 2 * owner + scalars_ref[1], hidden_ref[piece], total)
    high = total.astype(bf16)
    rows_ref[...] = total - high.astype(f32)
    out_ref[:count, :] = high
    out_ref[count:, :] = rows_ref[...].astype(bf16)


def collect(scalars, vectors, hidden):
    pieces, _, half = hidden.shape
    count = 2 * (len(vectors) + pieces)
    whole = pl.BlockSpec(memory_space=pltpu.VMEM)
    return pl.pallas_call(
        collect_kernel,
        in_specs=[pl.BlockSpec(memory_space=pltpu.SMEM)] + [whole] * (len(vectors) + 1),
        out_specs=whole,
        out_shape=jax.ShapeDtypeStruct((2 * count, half), bf16),
        scratch_shapes=[pltpu.VMEM((count, half), f32)],
        name="collect",
    )(scalars, *[vector[None] for vector in vectors], hidden)


def shift(value, by):
    size = lax.axis_size("tensor")
    return lax.ppermute(value, "tensor", [(i, (i + by) % size) for i in range(size)])


def swap(value):
    return lax.ppermute(value, "core", [(0, 1), (1, 0)])


def cross(value, axis, bit):
    size = lax.axis_size(axis)
    return lax.ppermute(value, axis, [(i, i ^ bit) for i in range(size)])


def order(flag, mine, other, axis):
    return jnp.concatenate(
        [jnp.where(flag == 0, mine, other), jnp.where(flag == 0, other, mine)], axis=axis
    )


def after(value, *others):
    return lax.optimization_barrier((value,) + others)[0]


def bits_of(axis):
    return [1 << place for place in range(lax.axis_size(axis).bit_length() - 1)]


def gather_step(held, bit, bits):
    flag = (lax.axis_index("quad") // bit) % 2
    return order(flag, held, cross(held, "quad", bit), len(bits) - bit.bit_length() + 1)


def scatter_cut(held, bit, bits):
    axis = len(bits) - bit.bit_length()
    flag = (lax.axis_index("quad") // bit) % 2
    keep = lax.dynamic_slice_in_dim(held, flag, 1, axis)
    return keep, lax.dynamic_slice_in_dim(held, 1 - flag, 1, axis)


def scatter_step(held, bit, bits):
    keep, send = scatter_cut(held, bit, bits)
    return keep, cross(send, "quad", bit)


def joined(pair):
    keep, other = pair
    return (keep.astype(f32) + other.astype(f32)).astype(bf16)


def sum_in_order(terms, owners):
    total = 0.0
    for place in range(len(terms)):
        term = terms[0]
        for owner, other in zip(owners[1:], terms[1:]):
            term = jnp.where(owner == place, other, term)
        total = total + term
    return total


def local(
    tokens,
    projections,
    query_bias,
    value_bias,
    mixer,
    mixer_bias,
    first_gain,
    first_shift,
    up_weight,
    up_bias,
    down_weight,
    down_bias,
    second_gain,
    second_shift,
    lengths,
    cotangent,
):
    row_count, features = tokens.shape
    columns = projections.shape[2]
    heads = columns // HEAD_DIM
    slots = lengths.shape[0]
    shards = lax.axis_size("tensor")
    quads = lax.axis_size("quad")
    per_share = row_count // shards
    mine = lax.axis_index("tensor")
    core = lax.axis_index("core")
    quad = lax.axis_index("quad")
    offset = mine * per_share
    hidden_count = up_weight.shape[1]
    half = hidden_count // 2
    bits = bits_of("quad")
    share = features // quads // 2

    def own(value):
        return lax.dynamic_slice_in_dim(value, offset, per_share, 0)

    up_half = lax.dynamic_slice_in_dim(up_weight, core * half, half, 1)
    down_half = lax.dynamic_slice_in_dim(down_weight, core * half, half, 0)
    up_rows, down_rows = features // quads, half // quads
    up_slice = lax.dynamic_slice_in_dim(up_half, quad * up_rows, up_rows, 0)
    down_slice = lax.dynamic_slice_in_dim(down_half, quad * down_rows, down_rows, 0)
    bundle = jnp.concatenate([up_slice.reshape(down_rows, -1), down_slice], axis=1)
    split = up_rows * half // down_rows
    mixer_rows = columns // 2
    bias_half = lax.dynamic_slice_in_dim(up_bias, core * half, half, 0)
    high = lax.reduce_precision(bias_half, 8, 7)
    middle = lax.reduce_precision(bias_half - high, 8, 7)
    low = bias_half - high - middle
    bias_rows = jnp.pad(
        jnp.stack([high, middle, low]).astype(bf16), ((0, 13), (0, features - half))
    )
    mixer_half = jnp.concatenate(
        [lax.dynamic_slice_in_dim(mixer, core * mixer_rows, mixer_rows, 0), bias_rows], axis=0
    )
    mixer_span = mixer_half.shape[0] // 2
    mixer_wide = jnp.concatenate([mixer_half[:mixer_span], mixer_half[mixer_span:]], axis=1)
    bundle = jnp.concatenate([bundle, mixer_wide], axis=0)
    bundles = [shift(bundle, k) for k in range(1, shards)]
    mixer_pieces = [mixer_half] + [
        jnp.concatenate([b[down_rows:, :features], b[down_rows:, features:]], axis=0)
        for b in bundles
    ]
    bundles = [b[:down_rows] for b in bundles]

    def padded(weight):
        shaped = weight.reshape(weight.shape[:-1] + (heads, HEAD_DIM))
        wide = jnp.pad(shaped, [(0, 0)] * (shaped.ndim - 1) + [(0, LANES - HEAD_DIM)])
        return wide.reshape(weight.shape[:-1] + (heads * LANES,))

    weight_wide = jnp.concatenate([padded(projections[i]) for i in range(3)], axis=1)
    bias_wide = jnp.concatenate(
        [padded(query_bias), jnp.zeros((heads * LANES,), f32), padded(value_bias)]
    )[None]
    scalars = jnp.concatenate([lengths, ((mine + 1) % shards).astype(jnp.int32).reshape(1)])
    query, key, key_t, value, rolled = prepare(
        scalars, tokens, weight_wide, bias_wide, heads, shards
    )
    spot = [(k - 1) % shards for k in range(shards)]
    span = row_count // 2
    mixed_first, kept_first = attend_forward(query, key_t, value, slots, 0, span)
    up_far = jnp.stack([b[:, :split].reshape(up_rows, half) for b in bundles])
    down_far = jnp.stack([b[:, split:] for b in bundles])
    ones = (1,) * len(bits)
    up_far = up_far.reshape((shards - 1,) + ones + (up_rows, half))
    down_far = down_far.reshape((shards - 1,) + ones + (down_rows, features))
    query = after(query, up_far, down_far)
    mixed_second, kept_second = attend_forward(query, key_t, value, slots, span, per_share)
    for place, (up_bit, down_bit) in enumerate(zip(bits, bits[::-1])):
        up_far, down_far = gather_step(up_far, up_bit, bits), gather_step(down_far, down_bit, bits)
        if place == 0:
            query = after(query, up_far, down_far)
    mixed_third, kept_third = attend_forward(
        query, key_t, value, slots, span + per_share, per_share
    )
    mixed_pieces = [mixed_first, mixed_second, mixed_third]
    mixed_out = jnp.concatenate(mixed_pieces, axis=0)
    query_kept = jnp.concatenate([kept_first, kept_second, kept_third], axis=0)
    sources = [mixed_first[:per_share], mixed_first[per_share:], mixed_second, mixed_third]
    mixed_in = [shift(sources[spot[k]], k) if k else sources[spot[k]] for k in range(shards)]
    up_all = (up_half, up_far.reshape(-1, features, half))
    down_all = (down_half, down_far.reshape(-1, half, features))
    mixed = jnp.concatenate(mixed_in, axis=1)
    mixer_stack = jnp.stack(mixer_pieces)
    bias_stack = mixer_stack[:, mixer_rows : mixer_rows + 3, :half].astype(f32)
    hidden_bias = (bias_stack[:, 0] + bias_stack[:, 1]) + bias_stack[:, 2]
    mixer_stack = mixer_stack[:, :mixer_rows]
    mixer_full = order(core, mixer_stack, swap(mixer_stack), 1).reshape(-1, features)

    attention = dot(mixed, mixer_full)
    first_normed, first_scale = normalize(own(tokens).astype(f32) + attention + mixer_bias)
    first = first_normed * first_gain + first_shift
    first_low = first.astype(bf16)
    first_other = swap(first_low)
    feature_half = features // 2
    weight_rows = jnp.concatenate([projections[i] for i in range(3)], axis=1)
    weight_own = lax.dynamic_slice_in_dim(weight_rows, core * feature_half, feature_half, 0)
    near = [k for k in range(1, shards) if k != shards // 2]
    weight_list = [weight_own] + [None] * (shards - 1)
    weight_list[near[0]] = shift(after(weight_own, first_low), near[0])
    hidden_bias = after(hidden_bias, weight_list[near[0]])
    active, slope, branch, branch_send = wide_forward(
        first_low, first_other, up_all, hidden_bias[:, None], down_all
    )
    branch = branch + swap(branch_send).astype(f32)
    second_normed, second_scale = normalize(first + branch + down_bias)
    layer_output = (second_normed * second_gain + second_shift).astype(bf16)

    places = offset + jnp.arange(per_share, dtype=jnp.int32)
    living = (places < jnp.sum(lengths)).astype(f32)
    incoming = own(cotangent).astype(f32) * living[:, None]
    second_back = norm_back(incoming, second_normed, second_scale, second_gain)
    second_low = second_back.astype(bf16)
    for k in near[1:]:
        weight_list[k] = shift(after(weight_own, weight_list[near[0]]), k)
        second_low = after(second_low, weight_list[k])
    second_other = swap(second_low)
    up_part, down_part, hidden_sum, first_part, first_send = wide_backward(
        second_low, second_other, first_low, first_other, up_all, down_all, active, slope
    )
    weight_list[shards // 2] = shift(after(weight_own, weight_list[near[-1]]), shards // 2)
    up_part, weight_list[shards // 2] = lax.optimization_barrier(
        (up_part, weight_list[shards // 2])
    )
    blocks = (2,) * len(bits) + (features // quads,)
    up_keep, up_send = scatter_cut(up_part.reshape(blocks + (-1,)), bits[0], bits)
    up_come = cross(up_send, "quad", bits[0])
    first_back = second_back + first_part + swap(first_send).astype(f32)
    base_back = norm_back(first_back, first_normed, first_scale, first_gain)
    base_low = base_back.astype(bf16)
    mixed_back = contract_cols(base_low, mixer_full).astype(bf16)
    back_in = [mixed_back[:, :columns]] + [
        shift(mixed_back[:, k * columns : (k + 1) * columns], -k) for k in range(1, shards)
    ]
    back_all = [back_in[(p + 1) % shards] for p in range(shards)]

    def mixed_half(which):
        begin = [k * columns for k in range(shards)]
        return jnp.concatenate(
            [
                jnp.where(
                    which == 0,
                    mixed[:, at : at + mixer_rows],
                    mixed[:, at + mixer_rows : at + columns],
                )
                for at in begin
            ],
            axis=1,
        )

    mixer_send = contract_rows(base_low, mixed_half(1 - core)).astype(bf16)
    mixer_keep = contract_rows(base_low, mixed_half(core))
    mixer_part = (mixer_keep + swap(mixer_send).astype(f32)).astype(bf16)
    other_part = jnp.concatenate([down_part, mixer_part], axis=1)
    other_keep, other_send = scatter_cut(other_part.reshape(blocks + (-1,)), bits[-1], bits)
    other_come = cross(other_send, "quad", bits[-1])

    norm_terms = [
        jnp.sum(first_back * first_normed, axis=0),
        jnp.sum(first_back, axis=0),
        jnp.sum(base_back, axis=0),
        jnp.sum(incoming * second_normed, axis=0),
        jnp.sum(incoming, axis=0),
        jnp.sum(second_back, axis=0),
    ]
    small_rows = collect(jnp.stack([mine, core]).astype(jnp.int32), norm_terms, hidden_sum)
    small_count = small_rows.shape[0] * small_rows.shape[1] // 2

    turns = [k for k in range(1, shards) if k != shards // 2] + [shards // 2, 0]
    pairs = [None] * shards
    come = [None] * shards
    more = (*back_all, after(mixed_out, up_send, other_send))
    for turn, k in enumerate(turns):
        query_now = query_kept
        if turn == 2:
            held = after((up_come, other_come), come[turns[0]])
            up_sum, other_sum = joined((up_keep, held[0])), joined((other_keep, held[1]))
            up_sum = scatter_cut(up_sum, bits[1], bits)
            other_sum = scatter_cut(other_sum, bits[-2], bits)
            query_now = after(query_now, up_sum[1], other_sum[1])
            up_sum = (up_sum[0], cross(up_sum[1], "quad", bits[1]))
            other_sum = (other_sum[0], cross(other_sum[1], "quad", bits[-2]))
        if turn == 3:
            query_now = after(query_now, come[turns[1]])
        query_sum, pairs[k], *kept = attend_backward(
            spot[k], shards, query_now, key, key_t, value, more, turn == shards - 1
        )
        if kept:
            transposed = kept
        more = (*transposed, query_sum)
        come[k] = pairs[k]
        if k:
            come[k] = shift(jnp.concatenate([pairs[k], small_rows], axis=0), k)
    query_all = query_sum
    pair_all = jnp.concatenate([pairs[(p + 1) % shards] for p in range(shards)], axis=0)
    for up_bit, other_bit in zip(bits[2:], bits[::-1][2:]):
        up_sum = scatter_step(joined(up_sum), up_bit, bits)
        other_sum = scatter_step(joined(other_sum), other_bit, bits)
    up_sum = joined(up_sum).reshape(features // quads, -1)
    other_sum = joined(other_sum).reshape(features // quads, -1)
    def piece_of(k):
        down_at, mixer_at = k * half, shards * half + k * mixer_rows
        return jnp.concatenate(
            [
                up_sum[:, k * half : (k + 1) * half],
                other_sum[:, down_at : down_at + half],
                other_sum[:, mixer_at : mixer_at + mixer_rows],
            ],
            axis=1,
        )

    total_pieces = [piece_of(k) for k in range(shards)]
    query_come = [query_all[spot[k] * per_share : (spot[k] + 1) * per_share] for k in range(shards)]
    total_come = total_pieces[:]
    ahead = come[shards // 2]
    for k in near:
        query_come[k] = shift(query_come[k], k)
    for k in near + [shards // 2]:
        total_come[k] = shift(total_pieces[k], -k)
    query_come[shards // 2] = shift(query_come[shards // 2], shards // 2)
    come = [after(piece, query_all) for piece in come]
    small_come = [small_rows] + [piece[per_share:] for piece in come[1:]]
    small_come = [piece.astype(f32).reshape(-1) for piece in small_come]
    small = sum_in_order(
        [piece[:small_count] + piece[small_count:] for piece in small_come],
        [(mine - k) % shards for k in range(shards)],
    )
    come = [piece[:per_share] for piece in come]
    weight_mine = jnp.concatenate(
        [piece[:, :columns] for piece in weight_list] + [piece[:, columns:] for piece in weight_list],
        axis=1,
    )
    weight_mine = after(weight_mine, pairs[turns[2]])
    weight_all = order(core, weight_mine, swap(weight_mine), 0)
    input_back = base_back + contract_cols(
        jnp.concatenate(come, axis=1), weight_all[:, features:]
    )
    input_back = input_back + contract_cols(
        jnp.concatenate(query_come, axis=1), weight_all[:, :features]
    )
    total = total_pieces[0].astype(f32)
    for k in range(1, shards):
        total = total + total_come[k].astype(f32)
    total = total.reshape(2, share, -1)
    keep = lax.dynamic_index_in_dim(total, core, 0, False)
    send = lax.dynamic_index_in_dim(total, 1 - core, 0, False)
    other = swap(send.astype(bf16)).astype(f32)

    def halves(begin, size):
        return order(core, keep[:, begin : begin + size], other[:, begin : begin + size], 1)

    up_weight_gradient = halves(0, half)
    down_weight_gradient = halves(half, half).T
    mixer_gradient = halves(2 * half, mixer_rows).T
    gradient = jnp.concatenate(
        [contract_rows(rolled, query_all), contract_rows(rolled, pair_all)], axis=1
    )
    sums = jnp.concatenate(
        [jnp.sum(query_all.astype(f32), axis=0), jnp.sum(pair_all.astype(f32), axis=0)]
    )

    width = sums.shape[0]
    count = -(-(width + small_count) // width)
    extra = 2 * count + (-2 * count) % 16
    sums = jnp.pad(jnp.concatenate([sums, small]), (0, count * width - width - small_count))
    sums = sums.reshape(count, width)

    def in_parts(sums):
        high = lax.reduce_precision(sums, 8, 7)
        return high, lax.reduce_precision(sums - high, 8, 7)

    def with_sums(rows, sums):
        parts = jnp.concatenate(in_parts(sums), axis=0).astype(bf16)
        parts = jnp.pad(parts, ((0, extra - 2 * count), (0, 0)))
        return jnp.concatenate([rows.astype(bf16), parts], axis=0)

    def rows_of(come):
        return come[:-extra].astype(f32)

    def sums_of(come):
        parts = come[-extra:].astype(f32)
        return parts[:count] + parts[count : 2 * count]

    gradient = gradient.reshape(quads, 2, share, -1)
    keep = lax.dynamic_index_in_dim(gradient, core, 1, False).reshape(quads * share, -1)
    send = lax.dynamic_index_in_dim(gradient, 1 - core, 1, False).reshape(quads * share, -1)
    other = swap(with_sums(send, sums))
    gradient = keep + rows_of(other)
    sums = sum(in_parts(sums)) + sums_of(other)
    if quads <= 4:
        pieces = [lax.dynamic_slice_in_dim(gradient, (quad ^ k) * share, share, 0) for k in range(quads)]
        arrived = [cross(with_sums(pieces[k], sums), "quad", k) for k in range(1, quads)]
        gradient = pieces[0] + sum(rows_of(piece) for piece in arrived)
        sums = sum_in_order(
            [sum(in_parts(sums))] + [sums_of(piece) for piece in arrived],
            [quad ^ k for k in range(quads)],
        )
    else:
        low_rows = jnp.concatenate(
            [with_sums(gradient[q * share : (q + 1) * share], sums) for q in range(quads)]
        ).reshape((2,) * len(bits) + (share + extra, -1))
        for bit in bits:
            low_rows = joined(scatter_step(low_rows, bit, bits))
        low_rows = low_rows.reshape(share + extra, -1)
        gradient, sums = rows_of(low_rows), sums_of(low_rows)
    sums = sums.reshape(-1)
    small = sums[width : width + small_count]
    projections_gradient = jnp.stack(
        [gradient[:, i * columns : (i + 1) * columns] for i in range(3)]
    )
    query_bias_gradient = sums[:columns]
    value_bias_gradient = sums[2 * columns : 3 * columns]
    (
        first_gain_gradient,
        first_shift_gradient,
        mixer_bias_gradient,
        second_gain_gradient,
        second_shift_gradient,
        down_bias_gradient,
    ) = [small[i * features : (i + 1) * features] for i in range(6)]
    up_bias_gradient = lax.dynamic_slice_in_dim(
        small, 6 * features + mine * hidden_count, hidden_count, 0
    )
    return (
        layer_output,
        input_back,
        projections_gradient,
        query_bias_gradient,
        value_bias_gradient,
        mixer_gradient,
        mixer_bias_gradient,
        first_gain_gradient,
        first_shift_gradient,
        up_weight_gradient,
        up_bias_gradient,
        down_weight_gradient,
        down_bias_gradient,
        second_gain_gradient,
        second_shift_gradient,
    )


def solution(mesh):
    dp, tensor = mesh.shape["dp"], mesh.shape["tensor"]
    inner = Mesh(mesh.devices.reshape(dp // 2, 2, tensor), ("quad", "core", "tensor"))
    rows = ("quad", "core")
    in_specs = (
        P(rows, None),
        P(None, None, "tensor"),
        P("tensor"),
        P("tensor"),
        P("tensor", None),
        P(),
        P(),
        P(),
        P(None, "tensor"),
        P("tensor"),
        P("tensor", None),
        P(),
        P(),
        P(),
        P(rows),
        P(rows, None),
    )
    out_specs = (
        P(("quad", "core", "tensor"), None),
        P(("quad", "core", "tensor"), None),
        P(None, rows, "tensor"),
        P("tensor"),
        P("tensor"),
        P("tensor", rows),
        P(),
        P(),
        P(),
        P(rows, "tensor"),
        P("tensor"),
        P("tensor", rows),
        P(),
        P(),
        P(),
    )
    return jax.shard_map(local, mesh=inner, in_specs=in_specs, out_specs=out_specs, check_vma=False)
```

```python
from functools import partial

import jax
import jax.numpy as jnp
from jax import lax
from jax.experimental import pallas as pl
from jax.experimental.pallas import tpu as pltpu
from jax.sharding import Mesh
from jax.sharding import PartitionSpec as P

HEAD_DIM = 64
LANES = 128
FACTOR = HEAD_DIM ** (-0.5)
epsilon = 1e-12
VMEM_BYTES = 32 * 1024 * 1024
WORK_SCALE = 1.0
f32 = jnp.float32
bf16 = jnp.bfloat16


def normalize(value):
    centre = value - jnp.mean(value, axis=1, keepdims=True)
    scale = lax.rsqrt(jnp.mean(centre * centre, axis=1, keepdims=True) + epsilon)
    return (centre * scale, scale)


def norm_back(incoming, normed, scale, gain):
    pushed = incoming * gain
    return scale * (
        pushed
        - jnp.mean(pushed, axis=1, keepdims=True)
        - normed * jnp.mean(pushed * normed, axis=1, keepdims=True)
    )


def dot(left, right):
    return jnp.dot(left, right, preferred_element_type=f32)


def contract_rows(left, right):
    return lax.dot_general(left, right, (((0,), (0,)), ((), ())), preferred_element_type=f32)


def contract_cols(left, right):
    return lax.dot_general(left, right, (((1,), (1,)), ((), ())), preferred_element_type=f32)


def work(microseconds):
    return pl.CostEstimate(
        flops=int(microseconds * WORK_SCALE * 1.15e9), bytes_accessed=0, transcendentals=0
    )


def three_parts(value):
    high = value.astype(bf16).astype(f32)
    rest = value - high
    middle = rest.astype(bf16).astype(f32)
    return high, middle, rest - middle


def prepare_kernel(
    scalars_ref, tokens_ref, weight_ref, bias_ref, q_ref, k_ref, kt_ref, v_ref, rolled_ref
):
    rows, width = q_ref.shape
    slots = scalars_ref.shape[0] - 1
    tokens = tokens_ref[...]
    rolled_ref[...] = tokens
    product = dot(tokens, weight_ref[...]) + bias_ref[...]
    part = lax.rem(scalars_ref[slots] + pl.program_id(0), pl.num_programs(0))
    place = lax.broadcasted_iota(jnp.int32, (rows, 1), 0) + part * rows
    segment = jnp.zeros((rows, 1), jnp.int32)
    end = jnp.int32(0)
    for slot in range(slots):
        end = end + scalars_ref[slot]
        segment = segment + (place >= end).astype(jnp.int32)
    count = slots + 1
    lane = lax.broadcasted_iota(jnp.int32, (rows, LANES), 1) - HEAD_DIM
    same = lane == segment
    in_mask = (lane >= 0) & (lane < count) & jnp.logical_not(same)
    in_sum = (lane >= count) & (lane < count + 3)
    query_more = jnp.where(same, 1.0, 0.0)
    key_more = jnp.where(in_mask, -1e30, jnp.where(in_sum, 1.0, 0.0))
    value_more = jnp.where((lane >= 0) & (lane < 3), 1.0, 0.0)
    for at in range(0, width, LANES):
        part = slice(at, at + LANES)
        query = jnp.where(lane < 0, product[:, part].astype(bf16).astype(f32) * FACTOR, query_more)
        key = jnp.where(lane < 0, product[:, width + at : width + at + LANES], key_more)
        value = jnp.where(
            lane < 0, product[:, 2 * width + at : 2 * width + at + LANES], value_more
        )
        q_ref[:, part] = query.astype(bf16)
        k_ref[:, part] = key.astype(bf16)
        kt_ref[part, :] = key.T.astype(bf16)
        v_ref[:, part] = value.astype(bf16)


def prepare(scalars, tokens, weight, bias, head_count, shards):
    row_count, features = tokens.shape
    width = head_count * LANES
    tile = row_count // shards
    here = lambda i, s: (i, 0)
    last = scalars.shape[0] - 1
    return pl.pallas_call(
        prepare_kernel,
        grid_spec=pltpu.PrefetchScalarGridSpec(
            num_scalar_prefetch=1,
            grid=(shards,),
            in_specs=[
                pl.BlockSpec((tile, features), lambda i, s: (lax.rem(s[last] + i, shards), 0)),
                pl.BlockSpec((features, 3 * width), lambda i, s: (0, 0)),
                pl.BlockSpec((1, 3 * width), lambda i, s: (0, 0)),
            ],
            out_specs=[
                pl.BlockSpec((tile, width), here),
                pl.BlockSpec((tile, width), here),
                pl.BlockSpec((width, tile), lambda i, s: (0, i)),
                pl.BlockSpec((tile, width), here),
                pl.BlockSpec((tile, features), here),
            ],
        ),
        out_shape=[
            jax.ShapeDtypeStruct((row_count, width), bf16),
            jax.ShapeDtypeStruct((row_count, width), bf16),
            jax.ShapeDtypeStruct((width, row_count), bf16),
            jax.ShapeDtypeStruct((row_count, width), bf16),
            jax.ShapeDtypeStruct((row_count, features), bf16),
        ],
        compiler_params=pltpu.CompilerParams(vmem_limit_bytes=VMEM_BYTES),
        cost_estimate=work(8),
        name="prepare",
    )(scalars, tokens, weight, bias)


def forward_kernel(slots, q_ref, kt_ref, v_ref, out_ref, kept_ref):
    rows, width = q_ref.shape
    heads = width // LANES
    lane = lax.broadcasted_iota(jnp.int32, (rows, LANES), 1) - HEAD_DIM - slots - 1
    for head in range(heads):
        part = slice(head * LANES, (head + 1) * LANES)
        query = q_ref[:, part]
        scores = dot(query, kt_ref[part, :])
        top = jnp.max(scores, axis=1, keepdims=True)
        weights = jnp.exp(scores - top).astype(bf16)
        mixed = dot(weights, v_ref[:, part])
        total = mixed[:, HEAD_DIM : HEAD_DIM + 1]
        out_ref[:, head * HEAD_DIM : (head + 1) * HEAD_DIM] = (
            mixed[:, :HEAD_DIM] / total
        ).astype(bf16)
        high, middle, low = three_parts(-(top + jnp.log(total)))
        extra = jnp.where(
            lane == 0, high, jnp.where(lane == 1, middle, jnp.where(lane == 2, low, 0.0))
        )
        kept_ref[:, part] = query + extra.astype(bf16)


def attend_forward(query, key_t, value, slots, begin, rows):
    row_count, width = query.shape
    heads = width // LANES
    tile = 256
    at = begin // tile
    return pl.pallas_call(
        partial(forward_kernel, slots),
        grid=(rows // tile,),
        in_specs=[
            pl.BlockSpec((tile, width), lambda i: (at + i, 0)),
            pl.BlockSpec((width, row_count), lambda i: (0, 0), pipeline_mode=pl.Buffered(1)),
            pl.BlockSpec((row_count, width), lambda i: (0, 0), pipeline_mode=pl.Buffered(1)),
        ],
        out_specs=[
            pl.BlockSpec((tile, heads * HEAD_DIM), lambda i: (i, 0)),
            pl.BlockSpec((tile, width), lambda i: (i, 0)),
        ],
        out_shape=[
            jax.ShapeDtypeStruct((rows, heads * HEAD_DIM), bf16),
            jax.ShapeDtypeStruct((rows, width), bf16),
        ],
        compiler_params=pltpu.CompilerParams(vmem_limit_bytes=VMEM_BYTES),
        cost_estimate=work(5 * rows // 512),
        name="attend_forward",
    )(query, key_t, value)


def backward_kernel(first, last, q_ref, k_ref, kt_ref, v_ref, *refs):
    if first:
        *g_refs, o_ref, dq_ref, pair_ref, gp, gt, qt, dqt, key_sum, value_sum, g_ref = refs
    elif last:
        gp, gt, qt, before_ref, dq_ref, pair_ref, dqt, key_sum, value_sum = refs
    else:
        gp, gt, qt, before_ref, dq_ref, pair_ref, dqt, key_sum, value_sum = refs
    rows, width = q_ref.shape
    keys = k_ref.shape[0]
    heads = width // LANES
    step = pl.program_id(0)
    if first:
        for place, source in enumerate(g_refs):

            @pl.when(step == place)
            def _():
                if source.shape == g_ref.shape:
                    g_ref[...] = source[...]
                else:
                    g_ref[: rows // 2, :] = source[:, : g_ref.shape[1]]
                    g_ref[rows // 2 :, :] = source[:, g_ref.shape[1] :]

        lane = lax.broadcasted_iota(jnp.int32, (rows, LANES), 1) - HEAD_DIM
        for head in range(heads):
            part = slice(head * LANES, (head + 1) * LANES)
            narrow = slice(head * HEAD_DIM, (head + 1) * HEAD_DIM)
            back = g_ref[:, narrow].astype(f32)
            mixed = o_ref[:, narrow].astype(f32)
            centre = -jnp.sum(back * mixed, axis=1, keepdims=True)
            high, middle, low = three_parts(centre)
            extra = jnp.where(
                lane == 0, high, jnp.where(lane == 1, middle, jnp.where(lane == 2, low, 0.0))
            )
            padded = jnp.concatenate([back, jnp.zeros_like(back)], axis=1) + extra
            gp[:, part] = padded.astype(bf16)
            gt[part, :] = padded.T.astype(bf16)
            qt[part, :] = q_ref[:, part].astype(f32).T.astype(bf16)
        dqt[...] = jnp.zeros_like(dqt)
    else:
        dqt[...] = before_ref[...]

    @pl.when(step == 0)
    def _():
        key_sum[...] = jnp.zeros_like(key_sum)
        value_sum[...] = jnp.zeros_like(value_sum)

    for head in range(heads):
        part = slice(head * LANES, (head + 1) * LANES)
        top = slice(head * LANES, head * LANES + HEAD_DIM)
        narrow = slice(head * HEAD_DIM, (head + 1) * HEAD_DIM)
        scores = dot(k_ref[:, part], qt[part, :])
        weights = jnp.exp(scores)
        pushed = dot(v_ref[:, part], gt[part, :])
        score_back = (weights * pushed).astype(bf16)
        value_sum[:, part] += dot(weights.astype(bf16), gp[:, part])
        key_sum[:, part] += dot(score_back, q_ref[:, part])
        dqt[narrow, :] += dot(kt_ref[top, :], score_back)
    if last:
        dq_ref[...] = (dqt[...] * FACTOR).T.astype(bf16)
    else:
        dq_ref[...] = dqt[...]

    @pl.when(step == pl.num_programs(0) - 1)
    def _():
        for head in range(heads):
            top = slice(head * LANES, head * LANES + HEAD_DIM)
            for at, total in enumerate((key_sum, value_sum)):
                place = (at * heads + head) * HEAD_DIM
                pair_ref[:, place : place + HEAD_DIM] = total[:, top].astype(bf16)


def attend_backward(place, count, query, key, key_t, value, more, last):
    row_count, width = query.shape
    heads = width // LANES
    narrow = heads * HEAD_DIM
    rows = row_count // count
    first = len(more) == count + 1
    down = lambda i: (i, 0)
    along = lambda i: (0, i)
    fixed = lambda i: (place, 0)
    in_specs = [
        pl.BlockSpec((rows, width), down),
        pl.BlockSpec((rows, width), fixed),
        pl.BlockSpec((width, rows), lambda i: (0, place)),
        pl.BlockSpec((rows, width), fixed),
    ]
    if first:
        in_specs += [pl.BlockSpec(piece.shape, lambda i: (0, 0)) for piece in more[:-1]]
        in_specs += [pl.BlockSpec((rows, narrow), down)]
    else:
        in_specs += [
            pl.BlockSpec((rows, width), down),
            pl.BlockSpec((width, rows), along),
            pl.BlockSpec((width, rows), along),
            pl.BlockSpec((narrow, rows), along),
        ]
    if last:
        out_specs = [pl.BlockSpec((rows, narrow), down)]
        out_shape = [jax.ShapeDtypeStruct((row_count, narrow), bf16)]
    else:
        out_specs = [pl.BlockSpec((narrow, rows), along)]
        out_shape = [jax.ShapeDtypeStruct((narrow, row_count), f32)]
    out_specs.append(pl.BlockSpec((rows, 2 * narrow), lambda i: (0, 0)))
    out_shape.append(jax.ShapeDtypeStruct((rows, 2 * narrow), bf16))
    if first:
        out_specs += [
            pl.BlockSpec((rows, width), down),
            pl.BlockSpec((width, rows), along),
            pl.BlockSpec((width, rows), along),
        ]
        out_shape += [
            jax.ShapeDtypeStruct((row_count, width), bf16),
            jax.ShapeDtypeStruct((width, row_count), bf16),
            jax.ShapeDtypeStruct((width, row_count), bf16),
        ]
    return pl.pallas_call(
        partial(backward_kernel, first, last),
        grid=(count,),
        in_specs=in_specs,
        out_specs=out_specs,
        out_shape=out_shape,
        scratch_shapes=[
            pltpu.VMEM((narrow, rows), f32),
            pltpu.VMEM((rows, width), f32),
            pltpu.VMEM((rows, width), f32),
        ]
        + [pltpu.VMEM((rows, narrow), bf16)] * first,
        compiler_params=pltpu.CompilerParams(vmem_limit_bytes=VMEM_BYTES),
        cost_estimate=work(11),
        name="attend_backward",
    )(query, key, key_t, value, *more)


def gelu_parts(hidden):
    gate = 0.5 * (1.0 + lax.erf(hidden * 0.7071067811865476))
    slope = gate + hidden * (0.3989422804014327 * jnp.exp(-0.5 * hidden * hidden))
    return hidden * gate, slope


def wide_forward_kernel(
    mine_ref, other_ref, up_own, up_far, bias_ref, down_own, down_far, active_ref, slope_ref, out_ref, send_ref
):
    rows = mine_ref.shape[0]
    half = up_own.shape[1]
    totals = [None, None]
    for step in range(bias_ref.shape[0]):
        up = up_own[...] if step == 0 else up_far[step - 1]
        down = down_own[...] if step == 0 else down_far[step - 1]
        for at, x_ref in enumerate((mine_ref, other_ref)):
            hidden = dot(x_ref[...], up) + bias_ref[step]
            active, slope = gelu_parts(hidden)
            active = active.astype(bf16)
            place = (slice(at * rows, (at + 1) * rows), slice(step * half, (step + 1) * half))
            active_ref[place] = active
            slope_ref[place] = slope.astype(bf16)
            part = dot(active, down)
            totals[at] = part if step == 0 else totals[at] + part
    out_ref[...] = totals[0]
    send_ref[...] = totals[1].astype(bf16)


def wide_forward(mine, other, up, bias, down):
    rows, features = mine.shape
    pieces, _, half = bias.shape
    whole = pl.BlockSpec(memory_space=pltpu.VMEM)
    return pl.pallas_call(
        wide_forward_kernel,
        in_specs=[whole] * 7,
        out_specs=[whole] * 4,
        out_shape=[
            jax.ShapeDtypeStruct((2 * rows, pieces * half), bf16),
            jax.ShapeDtypeStruct((2 * rows, pieces * half), bf16),
            jax.ShapeDtypeStruct((rows, features), f32),
            jax.ShapeDtypeStruct((rows, features), bf16),
        ],
        compiler_params=pltpu.CompilerParams(vmem_limit_bytes=VMEM_BYTES),
        cost_estimate=work(14),
        name="wide_forward",
    )(mine, other, *up, bias, *down)


def wide_backward_kernel(
    g_mine, g_other, x_mine, x_other, up_own, up_far, down_own, down_far, active_ref, slope_ref, up_part, down_part, bias_part, out_ref, send_ref, gt, xt, hb
):
    rows = g_mine.shape[0]
    half = up_own.shape[1]
    for at, (g_ref, x_ref) in enumerate(((g_mine, x_mine), (g_other, x_other))):
        place = slice(at * rows, (at + 1) * rows)
        gt[:, place] = g_ref[...].astype(f32).T.astype(bf16)
        xt[:, place] = x_ref[...].astype(f32).T.astype(bf16)
    totals = [None, None]
    for step in range(bias_part.shape[0]):
        up = up_own[...] if step == 0 else up_far[step - 1]
        down = down_own[...] if step == 0 else down_far[step - 1]
        across = slice(step * half, (step + 1) * half)
        sums = 0.0
        for at, g_ref in enumerate((g_mine, g_other)):
            place = slice(at * rows, (at + 1) * rows)
            back = contract_cols(g_ref[...], down) * slope_ref[place, across].astype(f32)
            back = back.astype(bf16)
            hb[place, :] = back
            sums = sums + jnp.sum(back.astype(f32), axis=0, keepdims=True)
            part = contract_cols(back, up)
            totals[at] = part if step == 0 else totals[at] + part
        bias_part[step] = sums
        up_part[:, across] = dot(xt[...], hb[...]).astype(bf16)
        down_part[:, across] = dot(gt[...], active_ref[:, across]).astype(bf16)
    out_ref[...] = totals[0]
    send_ref[...] = totals[1].astype(bf16)


def wide_backward(g_mine, g_other, x_mine, x_other, up, down, active, slope):
    rows, features = g_mine.shape
    half = down[0].shape[0]
    pieces = active.shape[1] // half
    whole = pl.BlockSpec(memory_space=pltpu.VMEM)
    return pl.pallas_call(
        wide_backward_kernel,
        in_specs=[whole] * 10,
        out_specs=[whole] * 5,
        out_shape=[
            jax.ShapeDtypeStruct((features, pieces * half), bf16),
            jax.ShapeDtypeStruct((features, pieces * half), bf16),
            jax.ShapeDtypeStruct((pieces, 1, half), f32),
            jax.ShapeDtypeStruct((rows, features), f32),
            jax.ShapeDtypeStruct((rows, features), bf16),
        ],
        scratch_shapes=[
            pltpu.VMEM((features, 2 * rows), bf16),
            pltpu.VMEM((features, 2 * rows), bf16),
            pltpu.VMEM((2 * rows, half), bf16),
        ],
        compiler_params=pltpu.CompilerParams(vmem_limit_bytes=VMEM_BYTES),
        cost_estimate=work(22),
        name="wide_backward",
    )(g_mine, g_other, x_mine, x_other, *up, *down, active, slope)


def collect_kernel(scalars_ref, *refs):
    *norm_refs, hidden_ref, out_ref, rows_ref = refs
    half = out_ref.shape[1]
    count = out_ref.shape[0] // 2
    shards = hidden_ref.shape[0]
    rows_ref[...] = jnp.zeros_like(rows_ref)
    for at, ref in enumerate(norm_refs):
        for side in range(2):
            rows_ref[2 * at + side : 2 * at + side + 1, :] = ref[:, side * half : (side + 1) * half]
    line = lax.broadcasted_iota(jnp.int32, (count, half), 0) - 2 * len(norm_refs)
    total = rows_ref[...]
    for piece in range(shards):
        owner = lax.rem(scalars_ref[0] - piece + shards, shards)
        total = jnp.where(line == 2 * owner + scalars_ref[1], hidden_ref[piece], total)
    high = total.astype(bf16)
    rows_ref[...] = total - high.astype(f32)
    out_ref[:count, :] = high
    out_ref[count:, :] = rows_ref[...].astype(bf16)


def collect(scalars, vectors, hidden):
    pieces, _, half = hidden.shape
    count = 2 * (len(vectors) + pieces)
    whole = pl.BlockSpec(memory_space=pltpu.VMEM)
    return pl.pallas_call(
        collect_kernel,
        in_specs=[pl.BlockSpec(memory_space=pltpu.SMEM)] + [whole] * (len(vectors) + 1),
        out_specs=whole,
        out_shape=jax.ShapeDtypeStruct((2 * count, half), bf16),
        scratch_shapes=[pltpu.VMEM((count, half), f32)],
        name="collect",
    )(scalars, *[vector[None] for vector in vectors], hidden)


def shift(value, by):
    size = lax.axis_size("tensor")
    return lax.ppermute(value, "tensor", [(i, (i + by) % size) for i in range(size)])


def swap(value):
    return lax.ppermute(value, "core", [(0, 1), (1, 0)])


def cross(value, axis, bit):
    size = lax.axis_size(axis)
    return lax.ppermute(value, axis, [(i, i ^ bit) for i in range(size)])


def order(flag, mine, other, axis):
    return jnp.concatenate(
        [jnp.where(flag == 0, mine, other), jnp.where(flag == 0, other, mine)], axis=axis
    )


def after(value, *others):
    return lax.optimization_barrier((value,) + others)[0]


def folded(value):
    rows = value.shape[0] // 2
    return jnp.concatenate([value[:rows], value[rows:]], axis=1)


def unfolded(value):
    cols = value.shape[1] // 2
    return jnp.concatenate([value[:, :cols], value[:, cols:]], axis=0)


def bits_of(axis):
    return [1 << place for place in range(lax.axis_size(axis).bit_length() - 1)]


def gather_step(held, bit, bits):
    flag = (lax.axis_index("quad") // bit) % 2
    return order(flag, held, cross(held, "quad", bit), len(bits) - bit.bit_length() + 1)


def scatter_cut(held, bit, bits):
    axis = len(bits) - bit.bit_length()
    flag = (lax.axis_index("quad") // bit) % 2
    keep = lax.dynamic_slice_in_dim(held, flag, 1, axis)
    return keep, lax.dynamic_slice_in_dim(held, 1 - flag, 1, axis)


def scatter_step(held, bit, bits):
    keep, send = scatter_cut(held, bit, bits)
    return keep, cross(send, "quad", bit)


def joined(pair):
    keep, other = pair
    return (keep.astype(f32) + other.astype(f32)).astype(bf16)


def sum_in_order(terms, owners):
    total = 0.0
    for place in range(len(terms)):
        term = terms[0]
        for owner, other in zip(owners[1:], terms[1:]):
            term = jnp.where(owner == place, other, term)
        total = total + term
    return total


def local(
    tokens,
    projections,
    query_bias,
    value_bias,
    mixer,
    mixer_bias,
    first_gain,
    first_shift,
    up_weight,
    up_bias,
    down_weight,
    down_bias,
    second_gain,
    second_shift,
    lengths,
    cotangent,
):
    row_count, features = tokens.shape
    columns = projections.shape[2]
    heads = columns // HEAD_DIM
    slots = lengths.shape[0]
    shards = lax.axis_size("tensor")
    quads = lax.axis_size("quad")
    per_share = row_count // shards
    mine = lax.axis_index("tensor")
    core = lax.axis_index("core")
    quad = lax.axis_index("quad")
    offset = mine * per_share
    hidden_count = up_weight.shape[1]
    half = hidden_count // 2
    bits = bits_of("quad")
    share = features // quads // 2

    def own(value):
        return lax.dynamic_slice_in_dim(value, offset, per_share, 0)

    up_half = lax.dynamic_slice_in_dim(up_weight, core * half, half, 1)
    down_half = lax.dynamic_slice_in_dim(down_weight, core * half, half, 0)
    up_rows, down_rows = features // quads, half // quads
    up_slice = lax.dynamic_slice_in_dim(up_half, quad * up_rows, up_rows, 0)
    down_slice = lax.dynamic_slice_in_dim(down_half, quad * down_rows, down_rows, 0)
    bundle = jnp.concatenate([up_slice.reshape(down_rows, -1), down_slice], axis=1)
    split = up_rows * half // down_rows
    mixer_rows = columns // 2
    bias_half = lax.dynamic_slice_in_dim(up_bias, core * half, half, 0)
    high = lax.reduce_precision(bias_half, 8, 7)
    middle = lax.reduce_precision(bias_half - high, 8, 7)
    low = bias_half - high - middle
    bias_rows = jnp.pad(
        jnp.stack([high, middle, low]).astype(bf16), ((0, 13), (0, features - half))
    )
    mixer_half = jnp.concatenate(
        [lax.dynamic_slice_in_dim(mixer, core * mixer_rows, mixer_rows, 0), bias_rows], axis=0
    )
    mixer_span = mixer_half.shape[0] // 2
    mixer_wide = jnp.concatenate([mixer_half[:mixer_span], mixer_half[mixer_span:]], axis=1)
    bundle = jnp.concatenate([bundle, mixer_wide], axis=0)
    bundles = [shift(bundle, k) for k in range(1, shards)]
    mixer_pieces = [mixer_half] + [
        jnp.concatenate([b[down_rows:, :features], b[down_rows:, features:]], axis=0)
        for b in bundles
    ]
    bundles = [b[:down_rows] for b in bundles]

    def padded(weight):
        shaped = weight.reshape(weight.shape[:-1] + (heads, HEAD_DIM))
        wide = jnp.pad(shaped, [(0, 0)] * (shaped.ndim - 1) + [(0, LANES - HEAD_DIM)])
        return wide.reshape(weight.shape[:-1] + (heads * LANES,))

    weight_wide = jnp.concatenate([padded(projections[i]) for i in range(3)], axis=1)
    bias_wide = jnp.concatenate(
        [padded(query_bias), jnp.zeros((heads * LANES,), f32), padded(value_bias)]
    )[None]
    scalars = jnp.concatenate([lengths, ((mine + 1) % shards).astype(jnp.int32).reshape(1)])
    query, key, key_t, value, rolled = prepare(
        scalars, tokens, weight_wide, bias_wide, heads, shards
    )
    spot = [(k - 1) % shards for k in range(shards)]
    span = row_count // 2
    mixed_first, kept_first = attend_forward(query, key_t, value, slots, 0, span)
    up_far = jnp.stack([b[:, :split].reshape(up_rows, half) for b in bundles])
    down_far = jnp.stack([b[:, split:] for b in bundles])
    ones = (1,) * len(bits)
    up_far = up_far.reshape((shards - 1,) + ones + (up_rows, half))
    down_far = down_far.reshape((shards - 1,) + ones + (down_rows, features))
    query = after(query, up_far, down_far)
    mixed_second, kept_second = attend_forward(query, key_t, value, slots, span, per_share)
    for place, (up_bit, down_bit) in enumerate(zip(bits, bits[::-1])):
        up_far, down_far = gather_step(up_far, up_bit, bits), gather_step(down_far, down_bit, bits)
        if place == 0:
            query = after(query, up_far, down_far)
    mixed_third, kept_third = attend_forward(
        query, key_t, value, slots, span + per_share, per_share
    )
    mixed_pieces = [mixed_first, mixed_second, mixed_third]
    mixed_out = jnp.concatenate(mixed_pieces, axis=0)
    query_kept = jnp.concatenate([kept_first, kept_second, kept_third], axis=0)
    sources = [mixed_first[:per_share], mixed_first[per_share:], mixed_second, mixed_third]
    mixed_in = [shift(sources[spot[k]], k) if k else sources[spot[k]] for k in range(shards)]
    up_all = (up_half, up_far.reshape(-1, features, half))
    down_all = (down_half, down_far.reshape(-1, half, features))
    mixed = jnp.concatenate(mixed_in, axis=1)
    mixer_stack = jnp.stack(mixer_pieces)
    bias_stack = mixer_stack[:, mixer_rows : mixer_rows + 3, :half].astype(f32)
    hidden_bias = (bias_stack[:, 0] + bias_stack[:, 1]) + bias_stack[:, 2]
    mixer_stack = mixer_stack[:, :mixer_rows]
    mixer_full = order(core, mixer_stack, swap(mixer_stack), 1).reshape(-1, features)

    attention = dot(mixed, mixer_full)
    first_normed, first_scale = normalize(own(tokens).astype(f32) + attention + mixer_bias)
    first = first_normed * first_gain + first_shift
    first_low = first.astype(bf16)
    first_other = swap(first_low)
    feature_half = features // 2
    weight_rows = jnp.concatenate([projections[i] for i in range(3)], axis=1)
    weight_own = lax.dynamic_slice_in_dim(weight_rows, core * feature_half, feature_half, 0)
    near = [k for k in range(1, shards) if k != shards // 2]
    weight_list = [weight_own] + [None] * (shards - 1)
    weight_list[near[0]] = shift(after(weight_own, first_low), near[0])
    hidden_bias = after(hidden_bias, weight_list[near[0]])
    active, slope, branch, branch_send = wide_forward(
        first_low, first_other, up_all, hidden_bias[:, None], down_all
    )
    branch = branch + swap(branch_send).astype(f32)
    second_normed, second_scale = normalize(first + branch + down_bias)
    layer_output = (second_normed * second_gain + second_shift).astype(bf16)

    places = offset + jnp.arange(per_share, dtype=jnp.int32)
    living = (places < jnp.sum(lengths)).astype(f32)
    incoming = own(cotangent).astype(f32) * living[:, None]
    second_back = norm_back(incoming, second_normed, second_scale, second_gain)
    second_low = second_back.astype(bf16)
    for k in near[1:]:
        weight_list[k] = shift(after(weight_own, weight_list[near[0]]), k)
        second_low = after(second_low, weight_list[k])
    second_other = swap(second_low)
    up_part, down_part, hidden_sum, first_part, first_send = wide_backward(
        second_low, second_other, first_low, first_other, up_all, down_all, active, slope
    )
    weight_list[shards // 2] = shift(after(weight_own, weight_list[near[-1]]), shards // 2)
    up_part, weight_list[shards // 2] = lax.optimization_barrier(
        (up_part, weight_list[shards // 2])
    )
    blocks = (2,) * len(bits) + (features // quads,)
    up_keep, up_send = scatter_cut(up_part.reshape(blocks + (-1,)), bits[0], bits)
    up_come = cross(up_send, "quad", bits[0])
    first_back = second_back + first_part + swap(first_send).astype(f32)
    base_back = norm_back(first_back, first_normed, first_scale, first_gain)
    base_low = base_back.astype(bf16)
    mixed_back = contract_cols(base_low, mixer_full).astype(bf16)
    back_in = [mixed_back[:, :columns]] + [
        shift(folded(mixed_back[:, k * columns : (k + 1) * columns]), -k) for k in range(1, shards)
    ]
    back_all = [back_in[(p + 1) % shards] for p in range(shards)]

    def mixed_half(which):
        begin = [k * columns for k in range(shards)]
        return jnp.concatenate(
            [
                jnp.where(
                    which == 0,
                    mixed[:, at : at + mixer_rows],
                    mixed[:, at + mixer_rows : at + columns],
                )
                for at in begin
            ],
            axis=1,
        )

    mixer_send = contract_rows(base_low, mixed_half(1 - core)).astype(bf16)
    mixer_keep = contract_rows(base_low, mixed_half(core))
    mixer_part = (mixer_keep + swap(mixer_send).astype(f32)).astype(bf16)
    other_part = jnp.concatenate([down_part, mixer_part], axis=1)
    other_keep, other_send = scatter_cut(other_part.reshape(blocks + (-1,)), bits[-1], bits)
    other_come = cross(other_send, "quad", bits[-1])

    norm_terms = [
        jnp.sum(first_back * first_normed, axis=0),
        jnp.sum(first_back, axis=0),
        jnp.sum(base_back, axis=0),
        jnp.sum(incoming * second_normed, axis=0),
        jnp.sum(incoming, axis=0),
        jnp.sum(second_back, axis=0),
    ]
    small_rows = collect(jnp.stack([mine, core]).astype(jnp.int32), norm_terms, hidden_sum)
    small_count = small_rows.shape[0] * small_rows.shape[1] // 2

    turns = [k for k in range(1, shards) if k != shards // 2] + [shards // 2, 0]
    pairs = [None] * shards
    come = [None] * shards
    more = (*back_all, after(mixed_out, up_send, other_send))
    for turn, k in enumerate(turns):
        query_now = query_kept
        if turn == 2:
            held = after((up_come, other_come), come[turns[0]])
            up_sum, other_sum = joined((up_keep, held[0])), joined((other_keep, held[1]))
            up_sum = scatter_cut(up_sum, bits[1], bits)
            other_sum = scatter_cut(other_sum, bits[-2], bits)
            query_now = after(query_now, up_sum[1], other_sum[1])
            up_sum = (up_sum[0], cross(up_sum[1], "quad", bits[1]))
            other_sum = (other_sum[0], cross(other_sum[1], "quad", bits[-2]))
        if turn == 3:
            query_now = after(query_now, come[turns[1]])
        query_sum, pairs[k], *kept = attend_backward(
            spot[k], shards, query_now, key, key_t, value, more, turn == shards - 1
        )
        if kept:
            transposed = kept
        more = (*transposed, query_sum)
        come[k] = pairs[k]
        if k:
            come[k] = shift(jnp.concatenate([pairs[k], small_rows], axis=0), k)
    query_all = query_sum
    pair_all = jnp.concatenate([pairs[(p + 1) % shards] for p in range(shards)], axis=0)
    for up_bit, other_bit in zip(bits[2:], bits[::-1][2:]):
        up_sum = scatter_step(joined(up_sum), up_bit, bits)
        other_sum = scatter_step(joined(other_sum), other_bit, bits)
    up_sum = joined(up_sum).reshape(features // quads, -1)
    other_sum = joined(other_sum).reshape(features // quads, -1)
    third = features // quads // 3

    def piece_of(k):
        mixer_at = shards * half + k * mixer_rows
        mixer_block = jnp.pad(
            other_sum[:, mixer_at : mixer_at + mixer_rows], ((0, 0), (0, LANES - mixer_rows))
        )
        return jnp.concatenate(
            [
                up_sum[:, k * half : (k + 1) * half],
                other_sum[:, k * half : (k + 1) * half],
                jnp.concatenate([mixer_block[at * third : (at + 1) * third] for at in range(3)], axis=1),
            ],
            axis=0,
        )

    total_pieces = [piece_of(k) for k in range(shards)]
    query_come = [query_all[spot[k] * per_share : (spot[k] + 1) * per_share] for k in range(shards)]
    total = total_pieces[0].astype(f32)
    for k in range(1, shards):
        arrived = shift(
            jnp.concatenate([folded(query_come[k]), total_pieces[shards - k]], axis=0), k
        )
        query_come[k] = unfolded(arrived[: per_share // 2])
        total = total + arrived[per_share // 2 :].astype(f32)
    come = [after(piece, query_all) for piece in come]
    small_come = [small_rows] + [piece[per_share:] for piece in come[1:]]
    small_come = [piece.astype(f32).reshape(-1) for piece in small_come]
    small = sum_in_order(
        [piece[:small_count] + piece[small_count:] for piece in small_come],
        [(mine - k) % shards for k in range(shards)],
    )
    come = [piece[:per_share] for piece in come]
    weight_mine = jnp.concatenate(
        [piece[:, :columns] for piece in weight_list] + [piece[:, columns:] for piece in weight_list],
        axis=1,
    )
    weight_mine = after(weight_mine, pairs[turns[2]])
    weight_all = order(core, weight_mine, swap(weight_mine), 0)
    input_back = base_back + contract_cols(
        jnp.concatenate(come, axis=1), weight_all[:, features:]
    )
    input_back = input_back + contract_cols(
        jnp.concatenate(query_come, axis=1), weight_all[:, :features]
    )
    held = features // quads
    mixer_block = jnp.concatenate(
        [total[2 * held :, at * LANES : at * LANES + mixer_rows] for at in range(3)], axis=0
    )
    total = jnp.concatenate([total[:held], total[held : 2 * held], mixer_block], axis=1)
    total = total.reshape(2, share, -1)
    keep = lax.dynamic_index_in_dim(total, core, 0, False)
    send = lax.dynamic_index_in_dim(total, 1 - core, 0, False)
    other = swap(send.astype(bf16)).astype(f32)

    def halves(begin, size):
        return order(core, keep[:, begin : begin + size], other[:, begin : begin + size], 1)

    up_weight_gradient = halves(0, half)
    down_weight_gradient = halves(half, half).T
    mixer_gradient = halves(2 * half, mixer_rows).T
    gradient = jnp.concatenate(
        [contract_rows(rolled, query_all), contract_rows(rolled, pair_all)], axis=1
    )
    sums = jnp.concatenate(
        [jnp.sum(query_all.astype(f32), axis=0), jnp.sum(pair_all.astype(f32), axis=0)]
    )

    width = sums.shape[0]
    count = -(-(width + small_count) // width)
    extra = 2 * count + (-2 * count) % 16
    sums = jnp.pad(jnp.concatenate([sums, small]), (0, count * width - width - small_count))
    sums = sums.reshape(count, width)

    def in_parts(sums):
        high = lax.reduce_precision(sums, 8, 7)
        return high, lax.reduce_precision(sums - high, 8, 7)

    def with_sums(rows, sums):
        parts = jnp.concatenate(in_parts(sums), axis=0).astype(bf16)
        parts = jnp.pad(parts, ((0, extra - 2 * count), (0, 0)))
        return jnp.concatenate([rows.astype(bf16), parts], axis=0)

    def rows_of(come):
        return come[:-extra].astype(f32)

    def sums_of(come):
        parts = come[-extra:].astype(f32)
        return parts[:count] + parts[count : 2 * count]

    gradient = gradient.reshape(quads, 2, share, -1)
    keep = lax.dynamic_index_in_dim(gradient, core, 1, False).reshape(quads * share, -1)
    send = lax.dynamic_index_in_dim(gradient, 1 - core, 1, False).reshape(quads * share, -1)
    other = swap(with_sums(send, sums))
    gradient = keep + rows_of(other)
    sums = sum(in_parts(sums)) + sums_of(other)
    if quads <= 4:
        pieces = [lax.dynamic_slice_in_dim(gradient, (quad ^ k) * share, share, 0) for k in range(quads)]
        arrived = [cross(with_sums(pieces[k], sums), "quad", k) for k in range(1, quads)]
        gradient = pieces[0] + sum(rows_of(piece) for piece in arrived)
        sums = sum_in_order(
            [sum(in_parts(sums))] + [sums_of(piece) for piece in arrived],
            [quad ^ k for k in range(quads)],
        )
    else:
        low_rows = jnp.concatenate(
            [with_sums(gradient[q * share : (q + 1) * share], sums) for q in range(quads)]
        ).reshape((2,) * len(bits) + (share + extra, -1))
        for bit in bits:
            low_rows = joined(scatter_step(low_rows, bit, bits))
        low_rows = low_rows.reshape(share + extra, -1)
        gradient, sums = rows_of(low_rows), sums_of(low_rows)
    sums = sums.reshape(-1)
    small = sums[width : width + small_count]
    projections_gradient = jnp.stack(
        [gradient[:, i * columns : (i + 1) * columns] for i in range(3)]
    )
    query_bias_gradient = sums[:columns]
    value_bias_gradient = sums[2 * columns : 3 * columns]
    (
        first_gain_gradient,
        first_shift_gradient,
        mixer_bias_gradient,
        second_gain_gradient,
        second_shift_gradient,
        down_bias_gradient,
    ) = [small[i * features : (i + 1) * features] for i in range(6)]
    up_bias_gradient = lax.dynamic_slice_in_dim(
        small, 6 * features + mine * hidden_count, hidden_count, 0
    )
    return (
        layer_output,
        input_back,
        projections_gradient,
        query_bias_gradient,
        value_bias_gradient,
        mixer_gradient,
        mixer_bias_gradient,
        first_gain_gradient,
        first_shift_gradient,
        up_weight_gradient,
        up_bias_gradient,
        down_weight_gradient,
        down_bias_gradient,
        second_gain_gradient,
        second_shift_gradient,
    )


def solution(mesh):
    dp, tensor = mesh.shape["dp"], mesh.shape["tensor"]
    inner = Mesh(mesh.devices.reshape(dp // 2, 2, tensor), ("quad", "core", "tensor"))
    rows = ("quad", "core")
    in_specs = (
        P(rows, None),
        P(None, None, "tensor"),
        P("tensor"),
        P("tensor"),
        P("tensor", None),
        P(),
        P(),
        P(),
        P(None, "tensor"),
        P("tensor"),
        P("tensor", None),
        P(),
        P(),
        P(),
        P(rows),
        P(rows, None),
    )
    out_specs = (
        P(("quad", "core", "tensor"), None),
        P(("quad", "core", "tensor"), None),
        P(None, rows, "tensor"),
        P("tensor"),
        P("tensor"),
        P("tensor", rows),
        P(),
        P(),
        P(),
        P(rows, "tensor"),
        P("tensor"),
        P("tensor", rows),
        P(),
        P(),
        P(),
    )
    return jax.shard_map(local, mesh=inner, in_specs=in_specs, out_specs=out_specs, check_vma=False)
```
